32 devices in a mesh: dp: 2 (over x), expert: 16 (over z, y, core).
Axes of the slice: x: 2, y: 2, z: 4, core: 2. Of those that a mesh axis runs over, the one named last changes fastest.
Arguments:
- tokens: bfloat16 [1024, 3584], P('expert'), may hold values from -6 to 6
- expert_ids: int32 [1024, 8], P('expert'), may hold values from 0 to 15, all different within a row; in each aligned block of 64 rows (0 to 63, 64 to 127, ...) at most 32 rows name the same one
- weight_num: int32 [1024, 8], P('expert'), may hold values from 64 to 1023
- gate_proj: bfloat16 [16, 3584, 2048], P('expert', None, 'dp'), may hold values from -0.09375 to 0.09375
- up_proj: bfloat16 [16, 3584, 2048], P('expert', None, 'dp'), may hold values from -0.09375 to 0.09375
- down_proj: bfloat16 [16, 2048, 3584], P('expert', 'dp'), may hold values from -0.125 to 0.125
Outputs:
- combined: bfloat16 [1024, 3584], P('expert', 'dp')
The draws below stay inside these ranges and needn't reach their ends.
Inputs may be any that keep to these rules, and one draw needn't show every extreme that they name: `expert_ids`: in the 64 rows of one device no expert is named by more than 32 rows, and some device has an expert named by exactly 32 of its rows.
All inputs are finite; a program needn't handle non-finite values.
Results may differ from the reference program's by a relative error of at most 0.015.
Values may be sent and summed in bfloat16 or wider, within the bound.
No kernel may reach another device: no remote copies, remote signals or barrier semaphores. Data moves between devices by JAX's collectives and lax.ppermute only.
A program may use at most 192 MiB of HBM per device.

```python
import math
import jax
import jax.numpy as jnp
import numpy as np
from jax import lax

D = 3584
F = 2048
TOP = 8
TOK_DEV = 64
EXPERTS = 16
TOKENS = 1024
SHARE = 1024
CAP = 32
N_DP = 2
N_EXPERT = 16


def plant(drawn, own_key, smallest, largest):
    shape = drawn.shape
    place = [jax.random.randint(jax.random.fold_in(own_key, axis), (), 0, shape[axis]) for axis in range(len(shape))]
    drawn = drawn.at[tuple(place)].set(smallest)
    longest = shape.index(max(shape))
    place[longest] = (place[longest] + 1) % shape[longest]
    return drawn.at[tuple(place)].set(largest)


def levels(rng, shape, shards, low, high):
    factor_of = 1.0
    for dim, parts in shards:
        draws = jax.random.uniform(jax.random.fold_in(jax.random.fold_in(rng, 6), dim), (parts,), jnp.float32, low / len(shards), high / len(shards))
        factor_of = factor_of * jnp.repeat(jnp.exp(draws), shape[dim] // parts).reshape((-1,) + (1,) * (len(shape) - 1 - dim))
    return factor_of


def deal_out(stream_key, own, number, rows, amount, top, reach, lean):
    order = jax.random.permutation(stream_key, amount)
    packed, usual = load_shares(amount, rows * top, reach, lean, True), load_shares(amount, rows * top, reach, lean, False)
    places = jnp.arange(amount)

    def named(sizes, rotation):
        used = int((sizes > 0).sum())
        fixed = max(1, used // 4)
        passed = fixed + (places - fixed + rotation * (used - fixed)) % max(1, amount - fixed)
        return jnp.zeros((amount,), jnp.int32).at[order[jnp.where(places < fixed, places, passed)]].set(jnp.asarray(sizes, jnp.int32))

    sizes = jnp.where(number % 4 == 0, named(packed, number // 4), named(usual, number - number // 4 - 1))
    mixed = jax.random.permutation(jax.random.fold_in(own, 3), amount)
    source_of, sink = mixed[0:amount // 2 * 2:2], mixed[1:amount // 2 * 2:2]
    margin = jnp.minimum(sizes[source_of] - 1, reach - sizes[sink]) // 2
    margin = jnp.where((source_of == order[0]) | (sink == order[0]) | (sizes[sink] == 0), 0, jnp.maximum(margin, 0))
    passed = jax.random.randint(jax.random.fold_in(own, 4), (amount // 2,), 0, 1 << 20) % (margin + 1)
    sizes = sizes.at[source_of].add(-passed).at[sink].add(passed)
    members = jnp.searchsorted(jnp.cumsum(sizes), jnp.arange(rows * top), side="right").astype(jnp.int32)
    table = members.reshape(top, rows).T
    table = table[jax.random.permutation(jax.random.fold_in(own, 1), rows)]
    rotation = jax.random.randint(jax.random.fold_in(own, 2), (rows, 1), 0, top)
    return jnp.take_along_axis(table, (jnp.arange(top)[None, :] + rotation) % top, axis=1)


def load_shares(number_of, total, reach, slope, full):
    loads = [(1 << 20) // math.isqrt(grade ** slope) + 1 for grade in range(1, number_of + 1)]
    largest = reach if full else min(reach, max(-(-total // number_of), total * loads[0] // sum(loads)))
    least = 1 if total - largest >= number_of - 1 else 0
    holding, rest = [largest] + [least] * (number_of - 1), total - largest - least * (number_of - 1)
    while rest > 0:
        candidates = [i for i in range(1, number_of) if holding[i] < largest] or [i for i in range(1, number_of) if holding[i] < reach]
        mass, remaining = sum([loads[i] for i in candidates]), rest
        for i in candidates:
            more = min(reach - holding[i], max(1, remaining * loads[i] // mass), rest)
            holding[i] = holding[i] + more
            rest = rest - more
    return np.array(holding)


def centred(own_key, extent, scale, most, cuts=(), kind=jnp.bfloat16):
    array = scale * jax.random.normal(own_key, extent, jnp.float32)
    if cuts:
        array = array * levels(own_key, extent, cuts, -0.22, 0.18)
    return jnp.clip(array, -most, most).astype(kind)


def setup_inputs(seed: int = 0) -> dict:
    arg_keys = jax.random.split(jax.random.key(seed), 7)
    tokens = centred(arg_keys[0], (TOKENS, D), 1.0, 6.0, ((0, 16),))
    expert_ids_keys = jax.random.split(jax.random.fold_in(arg_keys[1], 1), TOKENS // TOK_DEV)
    expert_ids_turns = jax.random.permutation(jax.random.fold_in(arg_keys[1], 3), TOKENS // TOK_DEV)
    expert_ids = jax.vmap(lambda own, number: deal_out(jax.random.fold_in(arg_keys[1], 2), own, number, TOK_DEV, EXPERTS, TOP, CAP, 1))(expert_ids_keys, expert_ids_turns).reshape((TOKENS, TOP))
    weight_num = plant(jax.random.randint(arg_keys[2], (TOKENS, TOP), 64, 1024), jax.random.fold_in(arg_keys[2], 1), 64, 1023).astype(jnp.int32)
    gate_proj = centred(arg_keys[3], (EXPERTS, D, F), D ** -0.5, 0.09375, ((0, 16), (2, 2)))
    up_proj = centred(arg_keys[4], (EXPERTS, D, F), D ** -0.5, 0.09375, ((0, 16), (2, 2)))
    down_proj = centred(arg_keys[5], (EXPERTS, F, D), F ** -0.5, 0.125, ((0, 16), (1, 2)))
    return dict(tokens=tokens, expert_ids=expert_ids, weight_num=weight_num, gate_proj=gate_proj, up_proj=up_proj, down_proj=down_proj)


def routing_table(block_ids, expert_total, capacity):
    row_count = block_ids.shape[0]
    top_count = block_ids.shape[1]
    flat_ids = block_ids.reshape(-1)
    onehot = (flat_ids[:, None] == jnp.arange(expert_total, dtype=jnp.int32)[None, :]).astype(jnp.int32)
    before = jnp.cumsum(onehot, axis=0) - onehot
    position = jnp.sum(before * onehot, axis=1).astype(jnp.int32)
    target = (flat_ids * capacity + position).astype(jnp.int32)
    owners = jnp.full((expert_total * capacity,), row_count * top_count, jnp.int32)
    owners = owners.at[target].set(jnp.arange(row_count * top_count, dtype=jnp.int32))
    return target, owners


def reference(tokens, expert_ids, weight_num, gate_proj, up_proj, down_proj):
    blocks = N_EXPERT
    pairs = TOK_DEV * TOP
    owners = jax.vmap(lambda block_ids: routing_table(block_ids, EXPERTS, CAP)[1])(expert_ids.reshape(blocks, TOK_DEV, TOP))
    weights = weight_num.astype(jnp.float32) / 1024.0
    flat_weight = weights.reshape(blocks, pairs)
    block_start = (jnp.arange(blocks, dtype=jnp.int32) * TOK_DEV).astype(jnp.int32)

    def per_expert(accum_out, expert_index):
        slot_owner = lax.dynamic_slice_in_dim(owners, (expert_index * CAP).astype(jnp.int32), CAP, 1)
        usable = slot_owner < pairs
        safe_slot = jnp.where(usable, slot_owner, 0).astype(jnp.int32)
        token_rows = (block_start[:, None] + safe_slot // TOP).reshape(-1).astype(jnp.int32)
        slot_weight = (jnp.take_along_axis(flat_weight, safe_slot, axis=1) * usable.astype(jnp.float32)).reshape(-1)
        picked = tokens[token_rows]
        gate_out = jnp.dot(picked, gate_proj[expert_index], preferred_element_type=jnp.float32)
        up_out = jnp.dot(picked, up_proj[expert_index], preferred_element_type=jnp.float32)
        hidden = (jax.nn.silu(gate_out) * up_out).astype(jnp.bfloat16)
        down_rows = down_proj[expert_index]
        expert_out = jnp.zeros((token_rows.shape[0], D), jnp.float32)
        for share_index in range(N_DP):
            share_out = jnp.dot(hidden[:, share_index * SHARE:(share_index + 1) * SHARE], down_rows[share_index * SHARE:(share_index + 1) * SHARE, :], preferred_element_type=jnp.float32).astype(jnp.bfloat16)
            share_out = lax.optimization_barrier(share_out)
            expert_out = expert_out + share_out.astype(jnp.float32)
        accum_out = accum_out.at[token_rows].add(slot_weight[:, None] * expert_out)
        return accum_out, None

    accum_out, _ = lax.scan(per_expert, jnp.zeros((TOKENS, D), jnp.float32), jnp.arange(EXPERTS, dtype=jnp.int32))
    return accum_out.astype(jnp.bfloat16)
```

```python
import jax
import jax.numpy as jnp
from jax import lax
from jax.experimental import pallas as pl
from jax.experimental.pallas import tpu as pltpu
from jax.sharding import PartitionSpec as P

ROOM = 8
BF = jnp.bfloat16
F32 = jnp.float32


def routing_table(block_ids, expert_total, capacity):
    row_count = block_ids.shape[0]
    top_count = block_ids.shape[1]
    flat_ids = block_ids.reshape(-1)
    onehot = (flat_ids[:, None] == jnp.arange(expert_total, dtype=jnp.int32)[None, :]).astype(
        jnp.int32
    )
    before = jnp.cumsum(onehot, axis=0) - onehot
    position = jnp.sum(before * onehot, axis=1)
    target = flat_ids * capacity + position
    owners = jnp.full((expert_total * capacity,), row_count * top_count, jnp.int32)
    owners = owners.at[target].set(jnp.arange(row_count * top_count, dtype=jnp.int32))
    return (target, owners)


def any_mesh(tokens, expert_ids, weight_num, gate_proj, up_proj, down_proj):
    experts = lax.axis_size("expert")
    row_count, top_count = expert_ids.shape
    feature_width = tokens.shape[1]
    capacity = max(ROOM, (row_count * top_count + experts - 1) // experts)
    target, owners = routing_table(expert_ids, experts, capacity)
    usable = owners < row_count * top_count
    source_row = jnp.where(usable, owners // top_count, 0)
    outgoing = jnp.where(usable[:, None], tokens[source_row], jnp.zeros((), tokens.dtype))
    outgoing = outgoing.reshape(experts, capacity, feature_width)
    block_rows = lax.all_to_all(outgoing, "expert", split_axis=0, concat_axis=0, tiled=True)
    flat_rows = block_rows.reshape(-1, feature_width)
    gate_out = jnp.dot(flat_rows, gate_proj[0], preferred_element_type=F32)
    up_out = jnp.dot(flat_rows, up_proj[0], preferred_element_type=F32)
    hidden = (jax.nn.silu(gate_out) * up_out).astype(BF)
    share_out = jnp.dot(hidden, down_proj[0], preferred_element_type=F32).astype(BF)
    partial_value = share_out.reshape(block_rows.shape[0], block_rows.shape[1], feature_width)
    weights = weight_num.astype(F32) / 1024.0
    summed = lax.psum_scatter(partial_value, "dp", scatter_dimension=2, tiled=True)
    returned = lax.all_to_all(summed, "expert", split_axis=0, concat_axis=0, tiled=True)
    part_width = returned.shape[2]
    picked = returned.astype(F32).reshape(experts * capacity, part_width)[target].reshape(
        row_count, top_count, part_width
    )
    return jnp.sum(picked * weights[:, :, None], axis=1).astype(BF)


NZ, NY, NC = 4, 2, 2
KJ = [(k, j) for k in range(NZ) for j in range(NY)]


def swap_expert(value, flip):
    pairs = [(i, i ^ flip) for i in range(NZ * NY * NC)]
    return lax.ppermute(value, "expert", pairs)


def swap_z(value, k):
    return swap_expert(value, k * NY * NC)


def swap_y(value):
    return swap_expert(value, NC)


def swap_core(value):
    return swap_expert(value, 1)


def swap_x(value):
    return lax.ppermute(value, "dp", [(0, 1), (1, 0)])


def gate_up_kernel(x_ref, rows_m, rows_f, gate_m, gate_f, up_m, up_f, weight, out):
    del x_ref
    a, b = rows_m[...], rows_f[...]
    gate = jnp.dot(a, gate_m[0], preferred_element_type=F32)
    gate += jnp.dot(b, gate_f[0], preferred_element_type=F32)
    up = jnp.dot(a, up_m[0], preferred_element_type=F32)
    up += jnp.dot(b, up_f[0], preferred_element_type=F32)
    out[...] = (gate / (1.0 + jnp.exp(-gate)) * up * weight[...]).astype(BF)


def gate_up(x, rows_m, rows_f, gate, up, weight):
    rows, half = rows_m.shape
    width = gate.shape[2]
    tile = 256
    whole = pl.BlockSpec((rows, half), lambda n, x: (0, 0))
    mine = pl.BlockSpec((1, half, tile), lambda n, x: (0, x[0], n))
    far = pl.BlockSpec((1, half, tile), lambda n, x: (0, 1 - x[0], n))
    return pl.pallas_call(
        gate_up_kernel,
        out_shape=jax.ShapeDtypeStruct((rows, width), BF),
        grid_spec=pltpu.PrefetchScalarGridSpec(
            num_scalar_prefetch=1,
            grid=(width // tile,),
            in_specs=[whole, whole, mine, far, mine, far, pl.BlockSpec((rows, 1), lambda n, x: (0, 0))],
            out_specs=pl.BlockSpec((rows, tile), lambda n, x: (0, n)),
        ),
        compiler_params=pltpu.CompilerParams(vmem_limit_bytes=48 << 20),
        cost_estimate=pl.CostEstimate(
            flops=8 * rows * half * width, bytes_accessed=8 * half * width, transcendentals=rows * width
        ),
    )(x, rows_m, rows_f, gate, gate, up, up, weight)


def down_kernel(hidden, down, near, away):
    value = jnp.dot(hidden[...], down[0], preferred_element_type=F32).astype(BF)
    rows = near.shape[0]
    near[...] = value[:rows]
    away[...] = value[rows:]


def down(hidden, weights):
    rows, depth = hidden.shape
    width = weights.shape[2]
    tile = 512
    out = jax.ShapeDtypeStruct((rows // 2, width), BF)
    return pl.pallas_call(
        down_kernel,
        out_shape=(out, out),
        grid=(width // tile,),
        in_specs=[
            pl.BlockSpec((rows, depth), lambda n: (0, 0)),
            pl.BlockSpec((1, depth, tile), lambda n: (0, 0, n)),
        ],
        out_specs=[pl.BlockSpec((rows // 2, tile), lambda n: (0, n))] * 2,
        compiler_params=pltpu.CompilerParams(vmem_limit_bytes=48 << 20),
        cost_estimate=pl.CostEstimate(
            flops=2 * rows * depth * width, bytes_accessed=2 * depth * width, transcendentals=0
        ),
    )(hidden, weights)


def slots(table, expert, room):
    top = table.shape[2] // 2
    named = table[:, :, :top] == expert
    numerator = jnp.sum(jnp.where(named, table[:, :, top:], 0), axis=2)
    chosen = jnp.any(named, axis=2)
    rows = table.shape[1]
    before = jnp.arange(rows)[:, None] < jnp.arange(rows)[None, :]
    place = jnp.sum(jnp.where(chosen[:, :, None] & before[None], 1, 0), axis=1)
    onehot = (place[:, None, :] == jnp.arange(room)[None, :, None]) & chosen[:, None, :]
    weight = jnp.sum(jnp.where(onehot, numerator[:, None, :], 0), axis=2).astype(F32) / 1024.0
    return onehot, weight.reshape(-1, 1)


def diagonal(onehot):
    count, room, rows = onehot.shape
    same = jnp.eye(count, dtype=bool)
    return (onehot[:, :, None, :] & same[:, None, :, None]).astype(BF).reshape(count * room, count * rows)


def add(*values):
    total = values[0].astype(F32)
    for value in values[1:]:
        total = total + value.astype(F32)
    return total.astype(BF)


def block_mesh(tokens, expert_ids, weight_num, gate_proj, up_proj, down_proj):
    x = lax.axis_index("dp")
    me = lax.axis_index("expert")
    rows, width = tokens.shape
    half = width // 2
    room = rows * expert_ids.shape[1] // (NZ * NY * NC)

    info = lax.all_gather(jnp.concatenate([expert_ids, weight_num], axis=1), "expert")
    order = jnp.array([k * NY * NC + j * NC for k, j in KJ], jnp.int32) ^ me
    near_table, away_table = info[order], info[order ^ 1]
    near_mine, near_weight = slots(near_table, me, room)
    near_other, _ = slots(near_table, me ^ 1, room)
    _, away_weight = slots(away_table, me, room)
    pick_mine, pick_other = diagonal(near_mine), diagonal(near_other)
    weight = jnp.concatenate([near_weight, away_weight], axis=0)

    mine = lax.dynamic_slice_in_dim(tokens, x * half, half, 1)
    far = lax.dynamic_slice_in_dim(tokens, (1 - x) * half, half, 1)
    got_m, got_f = {(0, 0): mine}, {(0, 0): far}
    for k in range(1, NZ):
        got_m[k, 0] = swap_z(mine, k)
    got_m[0, 1] = swap_y(mine)
    got_f[0, 1] = swap_y(far)
    for k in range(1, NZ):
        got_m[k, 1] = swap_y(got_m[k, 0])
        got_f[k, 0] = swap_x(got_m[k, 0])
    for k in range(1, NZ):
        got_f[k, 1] = swap_x(got_m[k, 1])

    def chosen(got):
        blocks = jnp.concatenate([got[kj] for kj in KJ], axis=0)
        keep = jnp.dot(pick_mine, blocks, preferred_element_type=F32).astype(BF)
        give = jnp.dot(pick_other, blocks, preferred_element_type=F32).astype(BF)
        return jnp.concatenate([keep, swap_core(give)], axis=0)

    rows_m = chosen(got_m)
    rows_f = chosen(got_f)
    hidden = gate_up(x.reshape(1), rows_m, rows_f, gate_proj, up_proj, weight)
    near, away = down(hidden, down_proj)
    back = swap_core(away)

    spread = jnp.dot(pick_mine.T, near, preferred_element_type=F32)
    spread = (spread + jnp.dot(pick_other.T, back, preferred_element_type=F32)).astype(BF)
    spread = spread.reshape(NZ, NY, rows, width)
    spread_m = lax.dynamic_slice_in_dim(spread, x * half, half, 3)
    spread_f = lax.dynamic_slice_in_dim(spread, (1 - x) * half, half, 3)
    quarter = half // 2
    first, second = slice(0, quarter), slice(quarter, half)
    columns = []
    summed = {}
    for part in (slice(2, 4), slice(0, 2)):
        a = add(spread_m[part, :, :, first], swap_x(spread_f[part, :, :, first]))
        b_m = add(spread_m[part, 0, :, second], swap_y(spread_m[part, 1, :, second]))
        b_f = add(spread_f[part, 0, :, second], swap_y(spread_f[part, 1, :, second]))
        a = add(a[:, 0], swap_y(a[:, 1]))
        b = add(b_m, swap_x(b_f))
        for i, k in enumerate(range(part.start, part.stop)):
            summed[k, 0], summed[k, 1] = a[i], b[i]
    for q in range(2):
        terms = [summed[0, q]] + [swap_z(summed[k, q], k) for k in (2, 3, 1)]
        columns.append(add(*terms))
    return jnp.concatenate(columns, axis=1)


def solution(mesh):
    placed = (
        P("expert", None),
        P("expert", None),
        P("expert", None),
        P("expert", None, "dp"),
        P("expert", None, "dp"),
        P("expert", "dp", None),
    )
    blocked = mesh.shape["dp"] == 2 and mesh.shape["expert"] == NZ * NY * NC
    return jax.shard_map(
        block_mesh if blocked else any_mesh,
        mesh=mesh,
        in_specs=placed,
        out_specs=P("expert", "dp"),
        check_vma=False,
    )
```

```python
import jax
import jax.numpy as jnp
from jax import lax
from jax.experimental import pallas as pl
from jax.experimental.pallas import tpu as pltpu
from jax.sharding import PartitionSpec as P

ROOM = 8
BF = jnp.bfloat16
F32 = jnp.float32


def routing_table(block_ids, expert_total, capacity):
    row_count = block_ids.shape[0]
    top_count = block_ids.shape[1]
    flat_ids = block_ids.reshape(-1)
    onehot = (flat_ids[:, None] == jnp.arange(expert_total, dtype=jnp.int32)[None, :]).astype(
        jnp.int32
    )
    before = jnp.cumsum(onehot, axis=0) - onehot
    position = jnp.sum(before * onehot, axis=1)
    target = flat_ids * capacity + position
    owners = jnp.full((expert_total * capacity,), row_count * top_count, jnp.int32)
    owners = owners.at[target].set(jnp.arange(row_count * top_count, dtype=jnp.int32))
    return (target, owners)


def any_mesh(tokens, expert_ids, weight_num, gate_proj, up_proj, down_proj):
    experts = lax.axis_size("expert")
    row_count, top_count = expert_ids.shape
    feature_width = tokens.shape[1]
    capacity = max(ROOM, (row_count * top_count + experts - 1) // experts)
    target, owners = routing_table(expert_ids, experts, capacity)
    usable = owners < row_count * top_count
    source_row = jnp.where(usable, owners // top_count, 0)
    outgoing = jnp.where(usable[:, None], tokens[source_row], jnp.zeros((), tokens.dtype))
    outgoing = outgoing.reshape(experts, capacity, feature_width)
    block_rows = lax.all_to_all(outgoing, "expert", split_axis=0, concat_axis=0, tiled=True)
    flat_rows = block_rows.reshape(-1, feature_width)
    gate_out = jnp.dot(flat_rows, gate_proj[0], preferred_element_type=F32)
    up_out = jnp.dot(flat_rows, up_proj[0], preferred_element_type=F32)
    hidden = (jax.nn.silu(gate_out) * up_out).astype(BF)
    share_out = jnp.dot(hidden, down_proj[0], preferred_element_type=F32).astype(BF)
    partial_value = share_out.reshape(block_rows.shape[0], block_rows.shape[1], feature_width)
    weights = weight_num.astype(F32) / 1024.0
    summed = lax.psum_scatter(partial_value, "dp", scatter_dimension=2, tiled=True)
    returned = lax.all_to_all(summed, "expert", split_axis=0, concat_axis=0, tiled=True)
    part_width = returned.shape[2]
    picked = returned.astype(F32).reshape(experts * capacity, part_width)[target].reshape(
        row_count, top_count, part_width
    )
    return jnp.sum(picked * weights[:, :, None], axis=1).astype(BF)


NZ, NY, NC = 4, 2, 2
TABLE = 128
SMALL = 16
KJ = [(k, j) for k in range(NZ) for j in range(NY)]


def swap_expert(value, flip, name):
    pairs = [(i, i ^ flip) for i in range(NZ * NY * NC)]
    with jax.named_scope(name):
        return lax.ppermute(value, "expert", pairs)


def swap_z(value, k, name):
    return swap_expert(value, k * NY * NC, name)


def swap_y(value, name):
    return swap_expert(value, NC, name)


def swap_core(value, name):
    return swap_expert(value, 1, name)


def swap_x(value, name):
    with jax.named_scope(name):
        return lax.ppermute(value, "dp", [(0, 1), (1, 0)])


COST = pl.CostEstimate(flops=1, bytes_accessed=1, transcendentals=0)


def call(kernel, out, ins):
    spec = [
        pl.BlockSpec(memory_space=pltpu.SMEM if v.dtype == jnp.int32 else pltpu.VMEM) for v in ins
    ]
    return pl.pallas_call(
        kernel,
        out_shape=out,
        in_specs=spec,
        out_specs=jax.tree.map(lambda _: pl.BlockSpec(memory_space=pltpu.VMEM), out),
        compiler_params=pltpu.CompilerParams(vmem_limit_bytes=SMALL << 20),
        cost_estimate=COST,
    )(*ins)


def prepare(x, tokens, ids, numerators):
    rows, width = tokens.shape
    half = width // 2

    def kernel(x_ref, tokens_ref, ids_ref, numerators_ref, mine, whole):
        side = x_ref[0]
        near = tokens_ref[:, pl.ds(pl.multiple_of(side * half, 128), half)]
        mine[:, :half] = near
        whole[:, :half] = near
        whole[:, half + TABLE :] = tokens_ref[:, pl.ds(pl.multiple_of((1 - side) * half, 128), half)]
        column = lax.broadcasted_iota(jnp.int32, (TABLE, rows), 0)
        expert = jnp.where(column < TABLE // 2, column, column - TABLE // 2)
        total = jnp.zeros((TABLE, rows), jnp.int32)
        for k in range(ids_ref.shape[0]):
            total += jnp.where(expert == ids_ref[pl.ds(k, 1)], numerators_ref[pl.ds(k, 1)], 0)
        high = lax.shift_right_logical(total, 5)
        code = jnp.where(column < TABLE // 2, high, total - high * 32)
        table = code.astype(F32).T.astype(BF)
        mine[:, half:] = table
        whole[:, half : half + TABLE] = table

    out = (
        jax.ShapeDtypeStruct((rows, half + TABLE), BF),
        jax.ShapeDtypeStruct((rows, width + TABLE), BF),
    )
    vmem = pl.BlockSpec(memory_space=pltpu.VMEM)
    return pl.pallas_call(
        kernel,
        out_shape=out,
        in_specs=[pl.BlockSpec(memory_space=pltpu.SMEM), vmem, vmem, vmem],
        out_specs=(vmem, vmem),
        cost_estimate=COST,
    )(x.reshape(1), tokens, ids.T, numerators.T)


def lookup(table, expert):
    row = lax.broadcasted_iota(jnp.int32, (TABLE, TABLE), 0)
    whose = jnp.where(lax.broadcasted_iota(jnp.int32, (TABLE, TABLE), 1) == 0, expert, expert + 1 - 2 * (expert % 2))
    code = jnp.where(row == whose, 32.0, 0.0) + jnp.where(row == whose + TABLE // 2, 1.0, 0.0)
    return jnp.dot(table, code.astype(BF), preferred_element_type=F32)


def select(me, room, half, blocks):
    rows, full = blocks[0].shape
    count = len(blocks)

    def kernel(me_ref, *refs):
        keep, give, put_ref = refs[-3:]
        mine = me_ref[0]
        before = lax.broadcasted_iota(jnp.int32, (rows, rows), 1) < lax.broadcasted_iota(
            jnp.int32, (rows, rows), 0
        )
        before = jnp.where(before, 1.0, 0.0).astype(BF)
        slot = lax.broadcasted_iota(jnp.int32, (rows, 2 * room), 1)
        first = slot < room
        for b, ref in enumerate(refs[:count]):
            chosen = jnp.where(lookup(ref[:, half : half + TABLE], mine) > 0, 1.0, 0.0)
            place = jnp.dot(before, chosen.astype(BF), preferred_element_type=F32)
            want = jnp.where(first, place[:, :1], place[:, 1:2] + room)
            here = jnp.where(first, chosen[:, :1], chosen[:, 1:2])
            put = jnp.where(want == slot.astype(F32), here, 0.0)
            put_ref[b] = put.astype(BF)
            got = jnp.dot(put.T.astype(BF), ref[...], preferred_element_type=F32).astype(BF)
            keep[pl.ds(b * room, room)] = got[:room]
            give[pl.ds(b * room, room)] = got[room:]

    out = jax.ShapeDtypeStruct((count * room, full), BF)
    put = jax.ShapeDtypeStruct((count, rows, 2 * room), BF)
    return call(kernel, (out, out, put), [me.reshape(1), *blocks])


def select_far(put, blocks):
    rows, full = blocks[0].shape
    half = full - TABLE
    room = put.shape[2] // 2

    def kernel(put_ref, *refs):
        keep, give = refs[-2:]
        for b, ref in enumerate(refs[:-2]):
            pick = put_ref[b].astype(F32).T.astype(BF)
            got = jnp.dot(pick, ref[:, :half], preferred_element_type=F32).astype(BF)
            keep[pl.ds(b * room, room)] = got[:room]
            give[pl.ds(b * room, room)] = got[room:]

    out = jax.ShapeDtypeStruct((len(blocks) * room, half), BF)
    return call(kernel, (out, out), [put, *blocks])


def touch(*weights):
    def kernel(*refs):
        total = jnp.zeros((16, 128), F32)
        for ref in refs[:-1]:
            total += ref[0, :16, :128].astype(F32)
        refs[-1][...] = total

    return call(kernel, jax.ShapeDtypeStruct((16, 128), F32), weights)


def gate_up(scalars, keep, got, gate, up, part, first=()):
    rows = keep.shape[0]
    depth, width = gate.shape[1:]
    half = depth // 2
    tile = 256

    def kernel(scalar_ref, keep_ref, got_ref, gate_ref, up_ref, *refs):
        x = scalar_ref[0]
        near = pl.ds(pl.multiple_of(x * half, half), half)
        far = pl.ds(pl.multiple_of((1 - x) * half, half), half)
        both = lambda start, size: jnp.concatenate(
            [ref[:, start : start + size] for ref in (keep_ref, got_ref)], axis=0
        )
        if part == 2:
            table = jnp.concatenate([refs[2][...], refs[3][...]], axis=0)[:, half:]
        elif part == 0:
            table = both(half, TABLE)
        if part != 1:
            weight = lookup(table, scalar_ref[1])[:, :1] / 1024.0
        for n in range(width // tile):
            columns = pl.ds(n * tile, tile)

            def product(ref):
                if part == 1:
                    return jnp.dot(both(0, half), ref[0, near, columns], preferred_element_type=F32)
                if part == 2:
                    return jnp.dot(both(0, half), ref[0, far, columns], preferred_element_type=F32)
                value = jnp.dot(both(0, half), ref[0, near, columns], preferred_element_type=F32)
                return value + jnp.dot(
                    both(half + TABLE, half), ref[0, far, columns], preferred_element_type=F32
                )

            g, u = product(gate_ref), product(up_ref)
            if part == 1:
                refs[0][:, columns] = g
                refs[1][:, columns] = u
                continue
            if part == 2:
                g += refs[0][:, columns]
                u += refs[1][:, columns]
            refs[-1][:, columns] = (g / (1.0 + jnp.exp(-g)) * u * weight).astype(BF)

    shape = lambda kind: jax.ShapeDtypeStruct((2 * rows, width), kind)
    out = (shape(F32), shape(F32)) if part == 1 else shape(BF)
    return call(kernel, out, [scalars, keep, got, gate, up, *first])


def down(scalars, hidden, weights, quarter, *tokens):
    rows, depth = hidden.shape
    tile = weights.shape[2] // 4

    def kernel(scalar_ref, hidden_ref, down_ref, *refs):
        near, away = refs[-2:]
        x = scalar_ref[0]
        for n in range(2):
            side = x if n else 1 - x
            start = (2 * side + quarter) * tile
            weight = down_ref[0, :, pl.ds(pl.multiple_of(start, 128), tile)]
            value = jnp.dot(hidden_ref[...], weight, preferred_element_type=F32).astype(BF)
            near[n] = value[: rows // 2]
            away[n] = value[rows // 2 :]

    out = jax.ShapeDtypeStruct((2, rows // 2, tile), BF)
    return call(kernel, (out, out), [scalars, hidden, weights, *tokens])


def spread(put, near, back, quarter, split):
    rows, room = put.shape[1], put.shape[2] // 2
    width = near.shape[2]
    whole = jax.ShapeDtypeStruct((2, 2, rows, width), BF)
    part = jax.ShapeDtypeStruct((2, rows, width), BF)
    out = (part, part, whole) if split else (whole, whole)

    def kernel(put_ref, near_ref, back_ref, *refs):
        *give, keep = refs
        for h in range(2):
            for b, (k, j) in enumerate(KJ[:4]):
                place = pl.ds(b * room, room)
                value = jnp.concatenate([near_ref[h, place], back_ref[h, place]], axis=0)
                got = jnp.dot(put_ref[b], value, preferred_element_type=F32).astype(BF)
                stays, index = (h == 1, j) if quarter == 0 else (j == 0, h)
                if stays:
                    keep[k, index] = got
                elif split:
                    give[k][index] = got
                else:
                    give[0][k, index] = got

    return call(kernel, out, [put, near, back])


def in_order(values, earlier):
    return lax.optimization_barrier((*values, *earlier))[: len(values)]


def after(value, *earlier):
    return in_order((value,), earlier)[0]


def add(*values):
    total = values[0].astype(F32)
    for value in values[1:]:
        total = total + value.astype(F32)
    return total.astype(BF)


def block_mesh(tokens, expert_ids, weight_num, gate_proj, up_proj, down_proj):
    x = lax.axis_index("dp")
    me = lax.axis_index("expert")
    rows, width = tokens.shape
    half = width // 2
    room = rows * expert_ids.shape[1] // (NZ * NY * NC)

    scalars = jnp.stack([x, me])

    mine, whole = prepare(x, tokens, expert_ids, weight_num)
    w0y = swap_y(whole, "w0y")
    w1 = swap_z(whole, 1, "w1")
    m2 = swap_z(mine, 2, "m2")
    touched = touch(*in_order((gate_proj, up_proj, down_proj), (mine,)))
    w1, m2, w0y = in_order((w1, m2, w0y), (touched,))
    m2y = swap_y(m2, "m2y")
    f2 = swap_x(m2, "f2")
    m3 = swap_z(m2, 1, "m3")
    w1y = swap_y(after(w1, m3), "w1y")
    f3 = swap_x(m3, "f3")
    m3y = swap_y(m3, "m3y")
    f2y = swap_x(m2y, "f2y")
    f3y = swap_x(m3y, "f3y")

    keep, give, put_f = select(after(me, f2), room, half, [m2, m2y, m3, m3y])
    got = swap_core(give, "rows_m")
    first = gate_up(scalars, keep, got, gate_proj, up_proj, 1, ())
    keep_f, give_f = select_far(after(put_f, first[0]), [f2, f2y, f3, f3y])
    got_f = swap_core(give_f, "rows_f")
    keep_n, give, put_n = select(after(me, keep_f), room, half, [whole, w0y, w1, w1y])
    got_n = swap_core(give, "rows_n")
    hidden_f = gate_up(after(scalars, keep_n), keep_f, got_f, gate_proj, up_proj, 2, [*first, keep, got])
    near_a, away = down(scalars, hidden_f, down_proj, 0, touched)
    back = swap_core(away, "back_a")
    near_b, away = down(after(scalars, near_a), hidden_f, down_proj, 1)
    a2, a3, keep_a = spread(put_f, near_a, back, 0, True)
    back = swap_core(away, "back_b")
    b2, b3, keep_b = spread(after(put_f, keep_a), near_b, back, 1, True)
    hidden_n = gate_up(after(scalars, keep_b), keep_n, got_n, gate_proj, up_proj, 0)
    near_n, away = down(scalars, hidden_n, down_proj, 0)
    back_n = swap_core(away, "back_n")
    near_o, away = down(after(scalars, near_n), hidden_n, down_proj, 1)
    back_o = swap_core(away, "back_o")

    b3, a3 = swap_y(b3, "b3"), swap_x(a3, "a3")
    put_n = after(put_n, a3, b3)
    a3, b3 = add(keep_a[1], a3), add(keep_b[1], b3)
    n, keep_n = spread(put_n, near_n, back_n, 0, False)
    o, keep_o = spread(put_n, near_o, back_o, 1, False)
    a2, b2 = in_order((a2, b2), (a3, b3))
    n, o = in_order((n, o), (a3, b3))
    o, n = swap_y(o, "o"), swap_x(n, "n")
    b2, a2 = swap_y(b2, "b2"), swap_x(a2, "a2")
    p3, q3 = swap_y(a3[1], "p3"), swap_x(b3[0], "q3")
    a2, b2 = add(keep_a[0], a2), add(keep_b[0], b2)
    p2, q2 = swap_y(a2[1], "p2"), swap_x(b2[0], "q2")
    s3 = jnp.stack([add(a3[0], p3), add(b3[1], q3)])
    p2, q2 = in_order((p2, q2), (s3,))
    s3 = swap_z(s3, 3, "s3")
    s2 = jnp.stack([add(a2[0], p2), add(b2[1], q2)])
    n, o = in_order((n, o), (s2,))
    s2 = swap_z(s2, 2, "s2")
    n, o = add(keep_n, n), add(keep_o, o)
    np, nq = swap_y(n[:, 1], "np"), swap_x(o[:, 0], "nq")
    n = jnp.stack([add(n[:, 0], np), add(o[:, 1], nq)])
    s1 = swap_z(n[:, 1], 1, "s1")
    total = add(n[:, 0], s1, s2, s3)
    return jnp.concatenate([total[0], total[1]], axis=1)


def solution(mesh):
    placed = (
        P("expert", None),
        P("expert", None),
        P("expert", None),
        P("expert", None, "dp"),
        P("expert", None, "dp"),
        P("expert", "dp", None),
    )
    blocked = mesh.shape["dp"] == 2 and mesh.shape["expert"] == NZ * NY * NC
    return jax.shard_map(
        block_mesh if blocked else any_mesh,
        mesh=mesh,
        in_specs=placed,
        out_specs=P("expert", "dp"),
        check_vma=False,
    )
```

```python
import jax
import jax.numpy as jnp
from jax import lax
from jax.experimental import pallas as pl
from jax.experimental.pallas import tpu as pltpu
from jax.sharding import PartitionSpec as P

ROOM = 8
BF = jnp.bfloat16
F32 = jnp.float32


def routing_table(block_ids, expert_total, capacity):
    row_count = block_ids.shape[0]
    top_count = block_ids.shape[1]
    flat_ids = block_ids.reshape(-1)
    onehot = (flat_ids[:, None] == jnp.arange(expert_total, dtype=jnp.int32)[None, :]).astype(
        jnp.int32
    )
    before = jnp.cumsum(onehot, axis=0) - onehot
    position = jnp.sum(before * onehot, axis=1)
    target = flat_ids * capacity + position
    owners = jnp.full((expert_total * capacity,), row_count * top_count, jnp.int32)
    owners = owners.at[target].set(jnp.arange(row_count * top_count, dtype=jnp.int32))
    return (target, owners)


def any_mesh(tokens, expert_ids, weight_num, gate_proj, up_proj, down_proj):
    experts = lax.axis_size("expert")
    row_count, top_count = expert_ids.shape
    feature_width = tokens.shape[1]
    capacity = max(ROOM, (row_count * top_count + experts - 1) // experts)
    target, owners = routing_table(expert_ids, experts, capacity)
    usable = owners < row_count * top_count
    source_row = jnp.where(usable, owners // top_count, 0)
    outgoing = jnp.where(usable[:, None], tokens[source_row], jnp.zeros((), tokens.dtype))
    outgoing = outgoing.reshape(experts, capacity, feature_width)
    block_rows = lax.all_to_all(outgoing, "expert", split_axis=0, concat_axis=0, tiled=True)
    flat_rows = block_rows.reshape(-1, feature_width)
    gate_out = jnp.dot(flat_rows, gate_proj[0], preferred_element_type=F32)
    up_out = jnp.dot(flat_rows, up_proj[0], preferred_element_type=F32)
    hidden = (jax.nn.silu(gate_out) * up_out).astype(BF)
    share_out = jnp.dot(hidden, down_proj[0], preferred_element_type=F32).astype(BF)
    partial_value = share_out.reshape(block_rows.shape[0], block_rows.shape[1], feature_width)
    weights = weight_num.astype(F32) / 1024.0
    summed = lax.psum_scatter(partial_value, "dp", scatter_dimension=2, tiled=True)
    returned = lax.all_to_all(summed, "expert", split_axis=0, concat_axis=0, tiled=True)
    part_width = returned.shape[2]
    picked = returned.astype(F32).reshape(experts * capacity, part_width)[target].reshape(
        row_count, top_count, part_width
    )
    return jnp.sum(picked * weights[:, :, None], axis=1).astype(BF)


NZ, NY, NC = 4, 2, 2
TABLE = 128
SMALL = 16
KJ = [(k, j) for k in range(NZ) for j in range(NY)]


def swap_expert(value, flip, name):
    pairs = [(i, i ^ flip) for i in range(NZ * NY * NC)]
    with jax.named_scope(name):
        return lax.ppermute(value, "expert", pairs)


def swap_z(value, k, name):
    return swap_expert(value, k * NY * NC, name)


def swap_y(value, name):
    return swap_expert(value, NC, name)


def swap_core(value, name):
    return swap_expert(value, 1, name)


def swap_x(value, name):
    with jax.named_scope(name):
        return lax.ppermute(value, "dp", [(0, 1), (1, 0)])


COST = pl.CostEstimate(flops=1, bytes_accessed=1, transcendentals=0)
MUCH = pl.CostEstimate(flops=1 << 35, bytes_accessed=1, transcendentals=0)


def call(kernel, out, ins, cost=COST):
    spec = [
        pl.BlockSpec(memory_space=pltpu.SMEM if v.dtype == jnp.int32 else pltpu.VMEM) for v in ins
    ]
    return pl.pallas_call(
        kernel,
        out_shape=out,
        in_specs=spec,
        out_specs=jax.tree.map(lambda _: pl.BlockSpec(memory_space=pltpu.VMEM), out),
        compiler_params=pltpu.CompilerParams(vmem_limit_bytes=SMALL << 20),
        cost_estimate=cost,
    )(*ins)


def prepare(x, tokens, ids, numerators):
    rows, width = tokens.shape
    half = width // 2

    def kernel(x_ref, tokens_ref, ids_ref, numerators_ref, mine, whole):
        side = x_ref[0]
        near = tokens_ref[:, pl.ds(pl.multiple_of(side * half, 128), half)]
        mine[:, :half] = near
        whole[:, :half] = near
        whole[:, half + TABLE :] = tokens_ref[:, pl.ds(pl.multiple_of((1 - side) * half, 128), half)]
        column = lax.broadcasted_iota(jnp.int32, (TABLE, rows), 0)
        expert = jnp.where(column < TABLE // 2, column, column - TABLE // 2)
        total = jnp.zeros((TABLE, rows), jnp.int32)
        for k in range(ids_ref.shape[0]):
            total += jnp.where(expert == ids_ref[pl.ds(k, 1)], numerators_ref[pl.ds(k, 1)], 0)
        high = lax.shift_right_logical(total, 5)
        code = jnp.where(column < TABLE // 2, high, total - high * 32)
        table = code.astype(F32).T.astype(BF)
        mine[:, half:] = table
        whole[:, half : half + TABLE] = table

    out = (
        jax.ShapeDtypeStruct((rows, half + TABLE), BF),
        jax.ShapeDtypeStruct((rows, width + TABLE), BF),
    )
    vmem = pl.BlockSpec(memory_space=pltpu.VMEM)
    return pl.pallas_call(
        kernel,
        out_shape=out,
        in_specs=[pl.BlockSpec(memory_space=pltpu.SMEM), vmem, vmem, vmem],
        out_specs=(vmem, vmem),
        cost_estimate=COST,
    )(x.reshape(1), tokens, ids.T, numerators.T)


def lookup(table, expert):
    row = lax.broadcasted_iota(jnp.int32, (TABLE, TABLE), 0)
    whose = jnp.where(lax.broadcasted_iota(jnp.int32, (TABLE, TABLE), 1) == 0, expert, expert + 1 - 2 * (expert % 2))
    code = jnp.where(row == whose, 32.0, 0.0) + jnp.where(row == whose + TABLE // 2, 1.0, 0.0)
    return jnp.dot(table, code.astype(BF), preferred_element_type=F32)


def select(me, room, half, blocks, cost=COST):
    rows, full = blocks[0].shape
    count = len(blocks)

    def kernel(me_ref, *refs):
        keep, give, put_ref = refs[-3:]
        mine = me_ref[0]
        before = lax.broadcasted_iota(jnp.int32, (rows, rows), 1) < lax.broadcasted_iota(
            jnp.int32, (rows, rows), 0
        )
        before = jnp.where(before, 1.0, 0.0).astype(BF)
        slot = lax.broadcasted_iota(jnp.int32, (rows, 2 * room), 1)
        first = slot < room
        chosen = [jnp.where(lookup(ref[:, half : half + TABLE], mine) > 0, 1.0, 0.0) for ref in refs[:count]]
        place = [jnp.dot(before, c.astype(BF), preferred_element_type=F32) for c in chosen]
        put = []
        for c, p in zip(chosen, place, strict=True):
            want = jnp.where(first, p[:, :1], p[:, 1:2] + room)
            here = jnp.where(first, c[:, :1], c[:, 1:2])
            put.append(jnp.where(want == slot.astype(F32), here, 0.0))
        pick = [p.T.astype(BF) for p in put]
        for b in range(count):
            put_ref[b] = put[b].astype(BF)
            got = jnp.dot(pick[b], refs[b][...], preferred_element_type=F32).astype(BF)
            keep[pl.ds(b * room, room)] = got[:room]
            give[pl.ds(b * room, room)] = got[room:]

    out = jax.ShapeDtypeStruct((count * room, full), BF)
    put = jax.ShapeDtypeStruct((count, rows, 2 * room), BF)
    return call(kernel, (out, out, put), [me.reshape(1), *blocks], cost)


def select_far(put, half, blocks):
    room = put.shape[2] // 2

    def kernel(put_ref, *refs):
        keep, give = refs[-2:]
        for b, ref in enumerate(refs[:-2]):
            pick = put_ref[b].astype(F32).T.astype(BF)
            got = jnp.dot(pick, ref[:, :half], preferred_element_type=F32).astype(BF)
            keep[pl.ds(b * room, room)] = got[:room]
            give[pl.ds(b * room, room)] = got[room:]

    out = jax.ShapeDtypeStruct((len(blocks) * room, half), BF)
    return call(kernel, (out, out), [put, *blocks])


def touch(*weights):
    def kernel(*refs):
        total = jnp.zeros((16, 128), F32)
        for ref in refs[:-1]:
            total += ref[0, :16, :128].astype(F32)
        refs[-1][...] = total

    return call(kernel, jax.ShapeDtypeStruct((16, 128), F32), weights)


def gate_up(scalars, keep, got, gate, up, part, first=(), tokens=()):
    rows = keep.shape[0]
    depth, width = gate.shape[1:]
    half = depth // 2
    tile = 256

    def kernel(scalar_ref, keep_ref, got_ref, gate_ref, up_ref, *refs):
        x = scalar_ref[0]
        near = pl.ds(pl.multiple_of(x * half, half), half)
        far = pl.ds(pl.multiple_of((1 - x) * half, half), half)
        both = lambda start, size: jnp.concatenate(
            [ref[:, start : start + size] for ref in (keep_ref, got_ref)], axis=0
        )
        if part == 2:
            table = jnp.concatenate([refs[2][...], refs[3][...]], axis=0)[:, half:]
        elif part == 0:
            table = both(half, TABLE)
        if part != 1:
            weight = lookup(table, scalar_ref[1])[:, :1] / 1024.0
        for n in range(width // tile):
            columns = pl.ds(n * tile, tile)

            def product(ref):
                if part == 1:
                    return jnp.dot(both(0, half), ref[0, near, columns], preferred_element_type=F32)
                if part == 2:
                    return jnp.dot(both(0, half), ref[0, far, columns], preferred_element_type=F32)
                value = jnp.dot(both(0, half), ref[0, near, columns], preferred_element_type=F32)
                return value + jnp.dot(
                    both(half + TABLE, half), ref[0, far, columns], preferred_element_type=F32
                )

            g, u = product(gate_ref), product(up_ref)
            if part == 1:
                refs[-2][:, columns] = g
                refs[-1][:, columns] = u
                continue
            if part == 2:
                g += refs[0][:, columns]
                u += refs[1][:, columns]
            refs[-1][:, columns] = (g / (1.0 + jnp.exp(-g)) * u * weight).astype(BF)

    shape = lambda kind: jax.ShapeDtypeStruct((2 * rows, width), kind)
    out = (shape(F32), shape(F32)) if part == 1 else shape(BF)
    return call(kernel, out, [scalars, keep, got, gate, up, *first, *tokens])


def down(scalars, hidden, weights, quarters, *tokens):
    rows, depth = hidden.shape
    tile = weights.shape[2] // 4

    def kernel(scalar_ref, hidden_ref, down_ref, *refs):
        near, away = refs[-2:]
        x = scalar_ref[0]
        for n in range(2 * len(quarters)):
            side = x if n % 2 else 1 - x
            start = (2 * side + quarters[n // 2]) * tile
            weight = down_ref[0, :, pl.ds(pl.multiple_of(start, 128), tile)]
            value = jnp.dot(hidden_ref[...], weight, preferred_element_type=F32).astype(BF)
            near[n] = value[: rows // 2]
            away[n] = value[rows // 2 :]

    out = jax.ShapeDtypeStruct((2 * len(quarters), rows // 2, tile), BF)
    return call(kernel, (out, out), [scalars, hidden, weights, *tokens])


def placed(put_ref, near_ref, back_ref, h, b):
    room = put_ref.shape[2] // 2
    part = pl.ds(b * room, room)
    value = jnp.concatenate([near_ref[h, part], back_ref[h, part]], axis=0)
    return jnp.dot(put_ref[b], value, preferred_element_type=F32).astype(BF)


def spread(put, near, back, quarter):
    rows, width = put.shape[1], near.shape[2]
    part = jax.ShapeDtypeStruct((2, rows, width), BF)
    whole = jax.ShapeDtypeStruct((2, 2, rows, width), BF)

    def kernel(put_ref, near_ref, back_ref, *refs):
        give, keep = refs[:2], refs[2]
        for h in range(2):
            for b, (k, j) in enumerate(KJ[:4]):
                got = placed(put_ref, near_ref, back_ref, h, b)
                stays, index = (h == 1, j) if quarter == 0 else (j == 0, h)
                if stays:
                    keep[k, index] = got
                else:
                    give[k][index] = got

    return call(kernel, (part, part, whole), [put, near, back])


def spread_own(put, near, back):
    rows, width = put.shape[1], near.shape[2]

    def kernel(put_ref, near_ref, back_ref, out):
        for h in range(near.shape[0]):
            for j in range(NY):
                out[h, j] = placed(put_ref, near_ref, back_ref, h, j)

    return call(kernel, jax.ShapeDtypeStruct((near.shape[0], NY, rows, width), BF), [put, near, back])


def in_order(values, earlier):
    return lax.optimization_barrier((*values, *earlier))[: len(values)]


def after(value, *earlier):
    return in_order((value,), earlier)[0]


def add(*values):
    total = values[0].astype(F32)
    for value in values[1:]:
        total = total + value.astype(F32)
    return total.astype(BF)


def block_mesh(tokens, expert_ids, weight_num, gate_proj, up_proj, down_proj):
    x = lax.axis_index("dp")
    me = lax.axis_index("expert")
    rows, width = tokens.shape
    half = width // 2
    room = rows * expert_ids.shape[1] // (NZ * NY * NC)

    scalars = jnp.stack([x, me])

    mine, whole = prepare(x, tokens, expert_ids, weight_num)
    w1 = swap_z(whole, 1, "w1")
    w0y = swap_y(whole, "w0y")
    m2 = swap_z(mine, 2, "m2")
    touched = touch(*in_order((gate_proj, up_proj), (mine,)))
    w0y, m2, _ = lax.optimization_barrier((w0y, m2, touched))
    w1y = swap_z(w0y, 1, "w1y")
    f2 = swap_x(m2, "f2")
    m2y = swap_y(m2, "m2y")
    m3 = swap_z(m2, 1, "m3")
    keep_0, give, put_0 = select(after(me, w1, m2), room, half, [whole, w0y], MUCH)
    got_0 = swap_core(after(give, f2), "rows_0")
    m3 = after(m3, m2y, f2)
    f3 = swap_x(m3, "f3")
    f2y = swap_x(after(m2y, m3), "f2y")
    m3y = swap_y(m3, "m3y")
    f3y = swap_x(m3y, "f3y")
    hidden_0 = gate_up(after(scalars, m3), keep_0, got_0, gate_proj, up_proj, 0)
    near_0, away = down(scalars, hidden_0, down_proj, (0, 1))
    back_0 = swap_core(away, "back_0")

    keep, give, put = select(after(me, near_0, f3, f2y, m3y), room, half, [m2, m2y, m3, m3y], MUCH)
    got = swap_core(give, "rows_m")
    keep_1, give, put_1 = select(after(me, keep), room, half, [w1, w1y])
    got_1 = swap_core(give, "rows_1")
    own = spread_own(after(put_0, keep_1), near_0, back_0)
    first = gate_up(after(scalars, own), keep, got, gate_proj, up_proj, 1)
    hidden_1 = gate_up(after(scalars, first[0]), keep_1, got_1, gate_proj, up_proj, 0)
    keep_f, give_f = select_far(after(put, hidden_1), half, [f2, f2y, f3, f3y])
    got_f = swap_core(give_f, "rows_f")
    near_1, away = down(after(scalars, keep_f), hidden_1, down_proj, (0, 1))
    back_1 = swap_core(away, "back_1")
    hidden = gate_up(after(scalars, near_1), keep_f, got_f, gate_proj, up_proj, 2, [*first, keep, got])
    near_a, away = down(scalars, hidden, down_proj, (0,), touched)
    back = swap_core(away, "back_a")
    n = spread_own(after(put_1, near_a), near_1, back_1)
    n0, n1 = swap_z(n[:2], 1, "n0"), swap_z(n[2:], 1, "n1")
    near_b, away = down(after(scalars, n), hidden, down_proj, (1,))
    a2, a3, keep_a = spread(put, near_a, back, 0)
    back = swap_core(away, "back_b")
    b2, b3, keep_b = spread(after(put, keep_a), near_b, back, 1)

    b3, a3 = swap_y(b3, "b3"), swap_x(a3, "a3")
    a3, b3 = add(keep_a[1], a3), add(keep_b[1], b3)
    a2, b2, a3, b3 = lax.optimization_barrier((a2, b2, a3, b3))
    b2, a2 = swap_y(b2, "b2"), swap_x(a2, "a2")
    p3, q3 = swap_y(a3[1], "p3"), swap_x(b3[0], "q3")
    s3 = jnp.stack([add(a3[0], p3), add(b3[1], q3)])
    n0, a2, b2 = in_order((n0, a2, b2), (s3,))
    s3 = swap_z(s3, 1, "s3")
    n0 = add(own[:2], n0)
    a2, b2 = in_order((a2, b2), (n0,))
    n, n0 = swap_x(n0[0], "n"), n0[1]
    a2, b2 = add(keep_a[0], a2), add(keep_b[0], b2)
    p2, q2 = swap_y(a2[1], "p2"), swap_x(b2[0], "q2")
    n1 = add(own[2:], after(n1, a2, b2))
    o, n1 = swap_y(n1[:, 1], "o"), n1[:, 0]
    s3, p2, q2 = in_order((s3, p2, q2), (n1,))
    s2 = jnp.stack([add(a2[0], p2, s3[0]), add(b2[1], q2, s3[1])])
    n, o = in_order((n, o), (s2,))
    s2 = swap_z(s2, 2, "s2")
    n, o = add(n0, n), add(n1, o)
    np, nq = swap_y(n[1], "np"), swap_x(o[0], "nq")
    n = jnp.stack([add(n[0], np), add(o[1], nq)])
    total = add(n, s2)
    return jnp.concatenate([total[0], total[1]], axis=1)


def solution(mesh):
    placed = (
        P("expert", None),
        P("expert", None),
        P("expert", None),
        P("expert", None, "dp"),
        P("expert", None, "dp"),
        P("expert", "dp", None),
    )
    blocked = mesh.shape["dp"] == 2 and mesh.shape["expert"] == NZ * NY * NC
    return jax.shard_map(
        block_mesh if blocked else any_mesh,
        mesh=mesh,
        in_specs=placed,
        out_specs=P("expert", "dp"),
        check_vma=False,
    )
```

```python
import jax
import jax.numpy as jnp
from jax import lax
from jax.experimental import pallas as pl
from jax.experimental.pallas import tpu as pltpu
from jax.sharding import PartitionSpec as P

ROOM = 8
BF = jnp.bfloat16
F32 = jnp.float32


def routing_table(block_ids, expert_total, capacity):
    row_count = block_ids.shape[0]
    top_count = block_ids.shape[1]
    flat_ids = block_ids.reshape(-1)
    onehot = (flat_ids[:, None] == jnp.arange(expert_total, dtype=jnp.int32)[None, :]).astype(
        jnp.int32
    )
    before = jnp.cumsum(onehot, axis=0) - onehot
    position = jnp.sum(before * onehot, axis=1)
    target = flat_ids * capacity + position
    owners = jnp.full((expert_total * capacity,), row_count * top_count, jnp.int32)
    owners = owners.at[target].set(jnp.arange(row_count * top_count, dtype=jnp.int32))
    return (target, owners)


def any_mesh(tokens, expert_ids, weight_num, gate_proj, up_proj, down_proj):
    experts = lax.axis_size("expert")
    row_count, top_count = expert_ids.shape
    feature_width = tokens.shape[1]
    capacity = max(ROOM, (row_count * top_count + experts - 1) // experts)
    target, owners = routing_table(expert_ids, experts, capacity)
    usable = owners < row_count * top_count
    source_row = jnp.where(usable, owners // top_count, 0)
    outgoing = jnp.where(usable[:, None], tokens[source_row], jnp.zeros((), tokens.dtype))
    outgoing = outgoing.reshape(experts, capacity, feature_width)
    block_rows = lax.all_to_all(outgoing, "expert", split_axis=0, concat_axis=0, tiled=True)
    flat_rows = block_rows.reshape(-1, feature_width)
    gate_out = jnp.dot(flat_rows, gate_proj[0], preferred_element_type=F32)
    up_out = jnp.dot(flat_rows, up_proj[0], preferred_element_type=F32)
    hidden = (jax.nn.silu(gate_out) * up_out).astype(BF)
    share_out = jnp.dot(hidden, down_proj[0], preferred_element_type=F32).astype(BF)
    partial_value = share_out.reshape(block_rows.shape[0], block_rows.shape[1], feature_width)
    weights = weight_num.astype(F32) / 1024.0
    summed = lax.psum_scatter(partial_value, "dp", scatter_dimension=2, tiled=True)
    returned = lax.all_to_all(summed, "expert", split_axis=0, concat_axis=0, tiled=True)
    part_width = returned.shape[2]
    picked = returned.astype(F32).reshape(experts * capacity, part_width)[target].reshape(
        row_count, top_count, part_width
    )
    return jnp.sum(picked * weights[:, :, None], axis=1).astype(BF)


NZ, NY, NC = 4, 2, 2
TABLE = 128
SMALL = 16
KJ = [(k, j) for k in range(NZ) for j in range(NY)]


def swap_expert(value, flip, name):
    pairs = [(i, i ^ flip) for i in range(NZ * NY * NC)]
    with jax.named_scope(name):
        return lax.ppermute(value, "expert", pairs)


def swap_z(value, k, name):
    return swap_expert(value, k * NY * NC, name)


def swap_y(value, name):
    return swap_expert(value, NC, name)


def swap_core(value, name):
    return swap_expert(value, 1, name)


def swap_x(value, name):
    with jax.named_scope(name):
        return lax.ppermute(value, "dp", [(0, 1), (1, 0)])


def swap_xy(value, first, name):
    pairs = []
    experts = NZ * NY * NC
    for x in range(2):
        for e in range(experts):
            along_x = (e % NC == 0) == first
            pairs.append((x * experts + e, (1 - x) * experts + e if along_x else x * experts + (e ^ NC)))
    with jax.named_scope(name):
        return lax.ppermute(value, ("dp", "expert"), pairs)


COST = pl.CostEstimate(flops=1, bytes_accessed=1, transcendentals=0)
MUCH = pl.CostEstimate(flops=1 << 35, bytes_accessed=1, transcendentals=0)


def call(kernel, out, ins, cost=COST):
    spec = [
        pl.BlockSpec(memory_space=pltpu.SMEM if v.dtype == jnp.int32 else pltpu.VMEM) for v in ins
    ]
    return pl.pallas_call(
        kernel,
        out_shape=out,
        in_specs=spec,
        out_specs=jax.tree.map(lambda _: pl.BlockSpec(memory_space=pltpu.VMEM), out),
        compiler_params=pltpu.CompilerParams(vmem_limit_bytes=SMALL << 20),
        cost_estimate=cost,
    )(*ins)


def prepare(x, tokens, ids, numerators):
    rows, width = tokens.shape
    half = width // 2

    def kernel(x_ref, tokens_ref, ids_ref, numerators_ref, mine, far):
        side = x_ref[0]
        mine[:, :half] = tokens_ref[:, pl.ds(pl.multiple_of(side * half, 128), half)]
        far[...] = tokens_ref[:, pl.ds(pl.multiple_of((1 - side) * half, 128), half)]
        column = lax.broadcasted_iota(jnp.int32, (TABLE, rows), 0)
        expert = jnp.where(column < TABLE // 2, column, column - TABLE // 2)
        total = jnp.zeros((TABLE, rows), jnp.int32)
        for k in range(ids_ref.shape[0]):
            total += jnp.where(expert == ids_ref[pl.ds(k, 1)], numerators_ref[pl.ds(k, 1)], 0)
        high = lax.shift_right_logical(total, 5)
        code = jnp.where(column < TABLE // 2, high, total - high * 32)
        mine[:, half:] = code.astype(F32).T.astype(BF)

    out = (
        jax.ShapeDtypeStruct((rows, half + TABLE), BF),
        jax.ShapeDtypeStruct((rows, half), BF),
    )
    vmem = pl.BlockSpec(memory_space=pltpu.VMEM)
    return pl.pallas_call(
        kernel,
        out_shape=out,
        in_specs=[pl.BlockSpec(memory_space=pltpu.SMEM), vmem, vmem, vmem],
        out_specs=(vmem, vmem),
        cost_estimate=COST,
    )(x.reshape(1), tokens, ids.T, numerators.T)


def lookup(table, expert):
    row = lax.broadcasted_iota(jnp.int32, (TABLE, TABLE), 0)
    whose = jnp.where(lax.broadcasted_iota(jnp.int32, (TABLE, TABLE), 1) == 0, expert, expert + 1 - 2 * (expert % 2))
    code = jnp.where(row == whose, 32.0, 0.0) + jnp.where(row == whose + TABLE // 2, 1.0, 0.0)
    return jnp.dot(table, code.astype(BF), preferred_element_type=F32)


def chooser(refs, layout, core):
    def read(n, columns=slice(None)):
        piece = layout[n]
        if isinstance(piece, tuple):
            return jnp.where(core == 0, refs[piece[0]][:, columns], refs[piece[1]][:, columns])
        return refs[piece][:, columns]

    return read


def flatten(pieces):
    arrays, layout = [], []

    def number(array):
        for n, other in enumerate(arrays):
            if other is array:
                return n
        arrays.append(array)
        return len(arrays) - 1

    for piece in pieces:
        layout.append(tuple(number(p) for p in piece) if isinstance(piece, tuple) else number(piece))
    return arrays, layout


def select(me, room, half, blocks, join=False, cost=COST):
    count = len(blocks)
    rows = blocks[0][0].shape[0]
    arrays, layout = flatten([piece for block in blocks for piece in block])
    widths = [arrays[n[0] if isinstance(n, tuple) else n].shape[1] for n in layout]
    start_of = [sum(len(block) for block in blocks[:b]) for b in range(count)]
    full = sum(widths[: len(blocks[0])])

    def kernel(me_ref, *refs):
        keep, give, put_ref = refs[-4:-1] if join else refs[-3:]
        mine = me_ref[0]
        read = chooser(refs, layout, mine % NC)
        before = lax.broadcasted_iota(jnp.int32, (rows, rows), 1) < lax.broadcasted_iota(
            jnp.int32, (rows, rows), 0
        )
        before = jnp.where(before, 1.0, 0.0).astype(BF)
        slot = lax.broadcasted_iota(jnp.int32, (rows, 2 * room), 1)
        first = slot < room
        tables = [read(n, slice(half, half + TABLE)) for n in start_of]
        chosen = [jnp.where(lookup(table, mine) > 0, 1.0, 0.0) for table in tables]
        place = [jnp.dot(before, c.astype(BF), preferred_element_type=F32) for c in chosen]
        put = []
        for c, p in zip(chosen, place, strict=True):
            want = jnp.where(first, p[:, :1], p[:, 1:2] + room)
            here = jnp.where(first, c[:, :1], c[:, 1:2])
            put.append(jnp.where(want == slot.astype(F32), here, 0.0))
        pick = [p.T.astype(BF) for p in put]
        for b in range(count):
            put_ref[b] = put[b].astype(BF)
            start = 0
            for n in range(start_of[b], start_of[b] + len(blocks[b])):
                columns = slice(start, start + widths[n])
                value = read(n)
                got = jnp.dot(pick[b], value, preferred_element_type=F32).astype(BF)
                keep[pl.ds(b * room, room), columns] = got[:room]
                give[pl.ds(b * room, room), columns] = got[room:]
                if join and b == count - 1:
                    refs[-1][:, columns] = value
                start += widths[n]

    out = jax.ShapeDtypeStruct((count * room, full), BF)
    put = jax.ShapeDtypeStruct((count, rows, 2 * room), BF)
    last = (jax.ShapeDtypeStruct((rows, full), BF),) if join else ()
    return call(kernel, (out, out, put, *last), [me.reshape(1), *arrays], cost)


def select_far(me, put, half, pieces):
    rows = put.shape[1]
    room = put.shape[2] // 2
    arrays, layout = flatten(pieces)

    def kernel(me_ref, put_ref, *refs):
        keep, give = refs[-2:]
        read = chooser(refs, layout, me_ref[0] % NC)
        for b in range(len(pieces)):
            pick = put_ref[b].astype(F32).T.astype(BF)
            got = jnp.dot(pick, read(b, slice(0, half)), preferred_element_type=F32).astype(BF)
            keep[pl.ds(b * room, room)] = got[:room]
            give[pl.ds(b * room, room)] = got[room:]

    out = jax.ShapeDtypeStruct((len(pieces) * room, half), BF)
    return call(kernel, (out, out), [me.reshape(1), put, *arrays])


def touch(*weights):
    def kernel(*refs):
        total = jnp.zeros((16, 128), F32)
        for ref in refs[:-1]:
            total += ref[0, :16, :128].astype(F32)
        refs[-1][...] = total

    return call(kernel, jax.ShapeDtypeStruct((16, 128), F32), weights)


def gate_up(scalars, keep, got, gate, up, part, first=(), tokens=()):
    rows = keep.shape[0]
    depth, width = gate.shape[1:]
    half = depth // 2
    tile = 256

    def kernel(scalar_ref, keep_ref, got_ref, gate_ref, up_ref, *refs):
        x = scalar_ref[0]
        near = pl.ds(pl.multiple_of(x * half, half), half)
        far = pl.ds(pl.multiple_of((1 - x) * half, half), half)
        both = lambda start, size: jnp.concatenate(
            [ref[:, start : start + size] for ref in (keep_ref, got_ref)], axis=0
        )
        if part == 2:
            table = jnp.concatenate([refs[2][...], refs[3][...]], axis=0)[:, half:]
        elif part == 0:
            table = both(half, TABLE)
        if part != 1:
            weight = lookup(table, scalar_ref[1])[:, :1] / 1024.0
        for n in range(width // tile):
            columns = pl.ds(n * tile, tile)

            def product(ref):
                if part == 1:
                    return jnp.dot(both(0, half), ref[0, near, columns], preferred_element_type=F32)
                if part == 2:
                    return jnp.dot(both(0, half), ref[0, far, columns], preferred_element_type=F32)
                value = jnp.dot(both(0, half), ref[0, near, columns], preferred_element_type=F32)
                return value + jnp.dot(
                    both(half + TABLE, half), ref[0, far, columns], preferred_element_type=F32
                )

            g, u = product(gate_ref), product(up_ref)
            if part == 1:
                refs[-2][:, columns] = g
                refs[-1][:, columns] = u
                continue
            if part == 2:
                g += refs[0][:, columns]
                u += refs[1][:, columns]
            refs[-1][:, columns] = (g / (1.0 + jnp.exp(-g)) * u * weight).astype(BF)

    shape = lambda kind: jax.ShapeDtypeStruct((2 * rows, width), kind)
    out = (shape(F32), shape(F32)) if part == 1 else shape(BF)
    return call(kernel, out, [scalars, keep, got, gate, up, *first, *tokens])


def down(scalars, hidden, weights, part, parts, *tokens):
    rows, depth = hidden.shape
    size = rows // 2 // parts
    tile = weights.shape[2] // 2

    def kernel(scalar_ref, hidden_ref, down_ref, *refs):
        near, away = refs[-2:]
        x = scalar_ref[0]
        value = jnp.concatenate(
            [hidden_ref[start : start + size] for start in (part * size, rows // 2 + part * size)], axis=0
        )
        for n in range(2):
            side = x if n else 1 - x
            weight = down_ref[0, :, pl.ds(pl.multiple_of(side * tile, 128), tile)]
            got = jnp.dot(value, weight, preferred_element_type=F32).astype(BF)
            near[n] = got[:size]
            away[n] = got[size:]

    out = jax.ShapeDtypeStruct((2, size, tile), BF)
    return call(kernel, (out, out), [scalars, hidden, weights, *tokens])


def spread(me, put, near, back, first, apart):
    rows, room = put.shape[1], put.shape[2] // 2
    width = near.shape[2]
    shape = lambda count: jax.ShapeDtypeStruct((count, rows, width), BF)

    def kernel(me_ref, put_ref, near_ref, back_ref, *outs):
        give, keep = (outs[0], outs[1]) if apart else (outs[0].at[0:2], outs[0].at[2:4])
        core = me_ref[0] % NC
        got = {}
        for h in range(2):
            for j in range(NY):
                part = pl.ds(j * room, room)
                value = jnp.concatenate([near_ref[h, part], back_ref[h, part]], axis=0)
                got[h, j] = jnp.dot(put_ref[first + j], value, preferred_element_type=F32).astype(BF)
        give[0] = jnp.where(core == 0, got[0, 0], got[1, 1])
        give[1] = got[0, 1]
        keep[0] = got[1, 0]
        keep[1] = jnp.where(core == 0, got[1, 1], got[0, 0])

    return call(kernel, (shape(2), shape(2)) if apart else shape(4), [me.reshape(1), put, near, back])


def in_order(values, earlier):
    return lax.optimization_barrier((*values, *earlier))[: len(values)]


def after(value, *earlier):
    return in_order((value,), earlier)[0]


def add(*values):
    total = values[0].astype(F32)
    for value in values[1:]:
        total = total + value.astype(F32)
    return total.astype(BF)


def block_mesh(tokens, expert_ids, weight_num, gate_proj, up_proj, down_proj):
    x = lax.axis_index("dp")
    me = lax.axis_index("expert")
    rows, width = tokens.shape
    half = width // 2
    room = rows * expert_ids.shape[1] // (NZ * NY * NC)

    scalars = jnp.stack([x, me])

    mine, far = prepare(x, tokens, expert_ids, weight_num)
    f1 = swap_z(far, 1, "f1")
    f0y = swap_y(far, "f0y")
    m1 = swap_z(mine, 1, "m1")
    m0y = swap_y(mine, "m0y")
    m2 = swap_z(mine, 2, "m2")
    touched = touch(*in_order((gate_proj, up_proj), (mine,)))
    f0y, m0y, m2, _ = lax.optimization_barrier((f0y, m0y, m2, touched))
    r2 = swap_xy(m2, False, "r2")
    q2 = swap_xy(m2, True, "q2")
    m3 = swap_z(m2, 1, "m3")
    keep_0, give, put_0, w0y = select(after(me, m2), room, half, [(mine, far), (m0y, f0y)], True, MUCH)
    got_0 = swap_core(after(give, q2, f1, m1), "rows_0")
    w1y = swap_z(w0y, 1, "w1y")
    q2, r2, m3 = lax.optimization_barrier((q2, r2, m3))
    t2 = swap_xy(q2, False, "t2")
    r3 = swap_xy(m3, False, "r3")
    q3 = swap_xy(m3, True, "q3")
    t3 = swap_xy(q3, False, "t3")
    hidden_0 = gate_up(after(scalars, m3), keep_0, got_0, gate_proj, up_proj, 0)
    near_0, away = down(scalars, hidden_0, down_proj, 0, 1)
    back_0 = swap_core(away, "back_0")

    blocks = [(m2,), ((r2, q2),), (m3,), ((r3, q3),)]
    keep, give, put = select(after(me, near_0, w1y, t2, r3, q3), room, half, blocks, False, MUCH)
    got = swap_core(give, "rows_m")
    keep_1, give, put_1 = select(after(me, keep), room, half, [(m1, f1), (w1y,)])
    got_1 = swap_core(give, "rows_1")
    first = gate_up(after(scalars, keep_1), keep, got, gate_proj, up_proj, 1)
    keep_f, give_f = select_far(me, after(put, first[0]), half, [(q2, r2), t2, (q3, r3), t3])
    got_f = swap_core(give_f, "rows_f")
    hidden_1 = gate_up(after(scalars, keep_f), keep_1, got_1, gate_proj, up_proj, 0)
    near_1, away = down(scalars, hidden_1, down_proj, 0, 1)
    back_1 = swap_core(away, "back_1")
    hidden = gate_up(after(scalars, near_1), keep_f, got_f, gate_proj, up_proj, 2, [*first, keep, got])
    near_3, away = down(scalars, hidden, down_proj, 1, 2, touched)
    back_3 = swap_core(away, "back_3")
    k1 = spread(me, after(put_1, near_3), near_1, back_1, 0, False)
    near_2, away = down(after(scalars, k1), hidden, down_proj, 0, 2)
    back_2 = swap_core(away, "back_2")
    give_3, keep_3 = spread(me, after(put, near_2), near_3, back_3, 2, True)
    give_2, keep_2 = spread(me, after(put, keep_3), near_2, back_2, 0, True)
    own = spread(me, after(put_0, keep_2), near_0, back_0, 0, False)

    n = swap_z(k1, 1, "n")
    u3 = swap_xy(give_3, True, "u3")
    u3 = add(keep_3, after(u3, keep_2))
    u2 = swap_xy(after(give_2, u3), True, "u2")
    v3 = swap_xy(u3[1], False, "v3")
    s3 = add(u3[0], v3)
    n = add(own, after(n, s3))
    u2 = after(u2, s3)
    s3 = swap_z(s3, 1, "s3")
    u2 = add(keep_2, u2)
    v2 = swap_xy(u2[1], False, "v2")
    s2 = add(u2[0], v2, s3)
    u0 = swap_xy(n[:2], True, "u0")
    s2 = swap_z(s2, 2, "s2")
    u0 = add(n[2:], u0)
    v0 = swap_xy(u0[1], False, "v0")
    return add(u0[0], v0, s2)


def solution(mesh):
    placed = (
        P("expert", None),
        P("expert", None),
        P("expert", None),
        P("expert", None, "dp"),
        P("expert", None, "dp"),
        P("expert", "dp", None),
    )
    blocked = mesh.shape["dp"] == 2 and mesh.shape["expert"] == NZ * NY * NC
    return jax.shard_map(
        block_mesh if blocked else any_mesh,
        mesh=mesh,
        in_specs=placed,
        out_specs=P("expert", "dp"),
        check_vma=False,
    )
```

```python
import jax
import jax.numpy as jnp
from jax import lax
from jax.experimental import pallas as pl
from jax.experimental.pallas import tpu as pltpu
from jax.sharding import PartitionSpec as P

ROOM = 8
BF = jnp.bfloat16
F32 = jnp.float32


def routing_table(block_ids, expert_total, capacity):
    row_count = block_ids.shape[0]
    top_count = block_ids.shape[1]
    flat_ids = block_ids.reshape(-1)
    onehot = (flat_ids[:, None] == jnp.arange(expert_total, dtype=jnp.int32)[None, :]).astype(
        jnp.int32
    )
    before = jnp.cumsum(onehot, axis=0) - onehot
    position = jnp.sum(before * onehot, axis=1)
    target = flat_ids * capacity + position
    owners = jnp.full((expert_total * capacity,), row_count * top_count, jnp.int32)
    owners = owners.at[target].set(jnp.arange(row_count * top_count, dtype=jnp.int32))
    return (target, owners)


def any_mesh(tokens, expert_ids, weight_num, gate_proj, up_proj, down_proj):
    experts = lax.axis_size("expert")
    row_count, top_count = expert_ids.shape
    feature_width = tokens.shape[1]
    capacity = max(ROOM, (row_count * top_count + experts - 1) // experts)
    target, owners = routing_table(expert_ids, experts, capacity)
    usable = owners < row_count * top_count
    source_row = jnp.where(usable, owners // top_count, 0)
    outgoing = jnp.where(usable[:, None], tokens[source_row], jnp.zeros((), tokens.dtype))
    outgoing = outgoing.reshape(experts, capacity, feature_width)
    block_rows = lax.all_to_all(outgoing, "expert", split_axis=0, concat_axis=0, tiled=True)
    flat_rows = block_rows.reshape(-1, feature_width)
    gate_out = jnp.dot(flat_rows, gate_proj[0], preferred_element_type=F32)
    up_out = jnp.dot(flat_rows, up_proj[0], preferred_element_type=F32)
    hidden = (jax.nn.silu(gate_out) * up_out).astype(BF)
    share_out = jnp.dot(hidden, down_proj[0], preferred_element_type=F32).astype(BF)
    partial_value = share_out.reshape(block_rows.shape[0], block_rows.shape[1], feature_width)
    weights = weight_num.astype(F32) / 1024.0
    summed = lax.psum_scatter(partial_value, "dp", scatter_dimension=2, tiled=True)
    returned = lax.all_to_all(summed, "expert", split_axis=0, concat_axis=0, tiled=True)
    part_width = returned.shape[2]
    picked = returned.astype(F32).reshape(experts * capacity, part_width)[target].reshape(
        row_count, top_count, part_width
    )
    return jnp.sum(picked * weights[:, :, None], axis=1).astype(BF)


NZ, NY, NC = 4, 2, 2
TABLE = 128
SMALL = 16
KJ = [(k, j) for k in range(NZ) for j in range(NY)]


def swap_expert(value, flip, name):
    pairs = [(i, i ^ flip) for i in range(NZ * NY * NC)]
    with jax.named_scope(name):
        return lax.ppermute(value, "expert", pairs)


def swap_z(value, k, name):
    return swap_expert(value, k * NY * NC, name)


def swap_y(value, name):
    return swap_expert(value, NC, name)


def swap_core(value, name):
    return swap_expert(value, 1, name)


def swap_x(value, name):
    with jax.named_scope(name):
        return lax.ppermute(value, "dp", [(0, 1), (1, 0)])


def swap_xy(value, first, name):
    pairs = []
    experts = NZ * NY * NC
    for x in range(2):
        for e in range(experts):
            along_x = (e % NC == 0) == first
            pairs.append((x * experts + e, (1 - x) * experts + e if along_x else x * experts + (e ^ NC)))
    with jax.named_scope(name):
        return lax.ppermute(value, ("dp", "expert"), pairs)


COST = pl.CostEstimate(flops=1, bytes_accessed=1, transcendentals=0)
MUCH = pl.CostEstimate(flops=1 << 35, bytes_accessed=1, transcendentals=0)


def call(kernel, out, ins, cost=COST):
    spec = [
        pl.BlockSpec(memory_space=pltpu.SMEM if v.dtype == jnp.int32 else pltpu.VMEM) for v in ins
    ]
    return pl.pallas_call(
        kernel,
        out_shape=out,
        in_specs=spec,
        out_specs=jax.tree.map(lambda _: pl.BlockSpec(memory_space=pltpu.VMEM), out),
        compiler_params=pltpu.CompilerParams(vmem_limit_bytes=SMALL << 20),
        cost_estimate=cost,
    )(*ins)


def prepare(x, tokens, ids, numerators):
    rows, width = tokens.shape
    half = width // 2

    def kernel(x_ref, tokens_ref, ids_ref, numerators_ref, mine, far):
        side = x_ref[0]
        mine[:, :half] = tokens_ref[:, pl.ds(pl.multiple_of(side * half, 128), half)]
        far[...] = tokens_ref[:, pl.ds(pl.multiple_of((1 - side) * half, 128), half)]
        column = lax.broadcasted_iota(jnp.int32, (TABLE, rows), 0)
        expert = jnp.where(column < TABLE // 2, column, column - TABLE // 2)
        total = jnp.zeros((TABLE, rows), jnp.int32)
        for k in range(ids_ref.shape[0]):
            total += jnp.where(expert == ids_ref[pl.ds(k, 1)], numerators_ref[pl.ds(k, 1)], 0)
        high = lax.shift_right_logical(total, 5)
        code = jnp.where(column < TABLE // 2, high, total - high * 32)
        mine[:, half:] = code.astype(F32).T.astype(BF)

    out = (
        jax.ShapeDtypeStruct((rows, half + TABLE), BF),
        jax.ShapeDtypeStruct((rows, half), BF),
    )
    vmem = pl.BlockSpec(memory_space=pltpu.VMEM)
    return pl.pallas_call(
        kernel,
        out_shape=out,
        in_specs=[pl.BlockSpec(memory_space=pltpu.SMEM), vmem, vmem, vmem],
        out_specs=(vmem, vmem),
        cost_estimate=COST,
    )(x.reshape(1), tokens, ids.T, numerators.T)


def lookup(table, expert):
    row = lax.broadcasted_iota(jnp.int32, (TABLE, TABLE), 0)
    whose = jnp.where(lax.broadcasted_iota(jnp.int32, (TABLE, TABLE), 1) == 0, expert, expert + 1 - 2 * (expert % 2))
    code = jnp.where(row == whose, 32.0, 0.0) + jnp.where(row == whose + TABLE // 2, 1.0, 0.0)
    return jnp.dot(table, code.astype(BF), preferred_element_type=F32)


def chooser(refs, layout, core):
    def read(n, columns=slice(None)):
        piece = layout[n]
        if isinstance(piece, tuple):
            return jnp.where(core == 0, refs[piece[0]][:, columns], refs[piece[1]][:, columns])
        return refs[piece][:, columns]

    return read


def flatten(pieces):
    arrays, layout = [], []

    def number(array):
        for n, other in enumerate(arrays):
            if other is array:
                return n
        arrays.append(array)
        return len(arrays) - 1

    for piece in pieces:
        layout.append(tuple(number(p) for p in piece) if isinstance(piece, tuple) else number(piece))
    return arrays, layout


def select(me, room, half, blocks, join=False, cost=COST):
    count = len(blocks)
    rows = blocks[0][0].shape[0]
    arrays, layout = flatten([piece for block in blocks for piece in block])
    widths = [arrays[n[0] if isinstance(n, tuple) else n].shape[1] for n in layout]
    start_of = [sum(len(block) for block in blocks[:b]) for b in range(count)]
    full = sum(widths[: len(blocks[0])])

    def kernel(me_ref, *refs):
        keep, give, put_ref = refs[-4:-1] if join else refs[-3:]
        mine = me_ref[0]
        read = chooser(refs, layout, mine % NC)
        before = lax.broadcasted_iota(jnp.int32, (rows, rows), 1) < lax.broadcasted_iota(
            jnp.int32, (rows, rows), 0
        )
        before = jnp.where(before, 1.0, 0.0).astype(BF)
        slot = lax.broadcasted_iota(jnp.int32, (rows, 2 * room), 1)
        first = slot < room
        tables = [read(n, slice(half, half + TABLE)) for n in start_of]
        chosen = [jnp.where(lookup(table, mine) > 0, 1.0, 0.0) for table in tables]
        place = [jnp.dot(before, c.astype(BF), preferred_element_type=F32) for c in chosen]
        put = []
        for c, p in zip(chosen, place, strict=True):
            want = jnp.where(first, p[:, :1], p[:, 1:2] + room)
            here = jnp.where(first, c[:, :1], c[:, 1:2])
            put.append(jnp.where(want == slot.astype(F32), here, 0.0))
        pick = [p.T.astype(BF) for p in put]
        for b in range(count):
            put_ref[b] = put[b].astype(BF)
            start = 0
            for n in range(start_of[b], start_of[b] + len(blocks[b])):
                columns = slice(start, start + widths[n])
                value = read(n)
                got = jnp.dot(pick[b], value, preferred_element_type=F32).astype(BF)
                keep[pl.ds(b * room, room), columns] = got[:room]
                give[pl.ds(b * room, room), columns] = got[room:]
                if join and b == count - 1:
                    refs[-1][:, columns] = value
                start += widths[n]

    out = jax.ShapeDtypeStruct((count * room, full), BF)
    put = jax.ShapeDtypeStruct((count, rows, 2 * room), BF)
    last = (jax.ShapeDtypeStruct((rows, full), BF),) if join else ()
    return call(kernel, (out, out, put, *last), [me.reshape(1), *arrays], cost)


def select_far(me, put, half, pieces):
    rows = put.shape[1]
    room = put.shape[2] // 2
    arrays, layout = flatten(pieces)

    def kernel(me_ref, put_ref, *refs):
        keep, give = refs[-2:]
        read = chooser(refs, layout, me_ref[0] % NC)
        for b in range(len(pieces)):
            pick = put_ref[b].astype(F32).T.astype(BF)
            got = jnp.dot(pick, read(b, slice(0, half)), preferred_element_type=F32).astype(BF)
            keep[pl.ds(b * room, room)] = got[:room]
            give[pl.ds(b * room, room)] = got[room:]

    out = jax.ShapeDtypeStruct((len(pieces) * room, half), BF)
    return call(kernel, (out, out), [me.reshape(1), put, *arrays])


def touch(*weights):
    def kernel(*refs):
        total = jnp.zeros((16, 128), F32)
        for ref in refs[:-1]:
            total += ref[0, :16, :128].astype(F32)
        refs[-1][...] = total

    return call(kernel, jax.ShapeDtypeStruct((16, 128), F32), weights)


def gate_up(scalars, keep, got, gate, up, part, first=(), tokens=()):
    rows = keep.shape[0]
    depth, width = gate.shape[1:]
    half = depth // 2
    tile = 256

    def kernel(scalar_ref, keep_ref, got_ref, gate_ref, up_ref, *refs):
        x = scalar_ref[0]
        near = pl.ds(pl.multiple_of(x * half, half), half)
        far = pl.ds(pl.multiple_of((1 - x) * half, half), half)
        both = lambda start, size: jnp.concatenate(
            [ref[:, start : start + size] for ref in (keep_ref, got_ref)], axis=0
        )
        if part == 2:
            table = jnp.concatenate([refs[2][...], refs[3][...]], axis=0)[:, half:]
        elif part == 0:
            table = both(half, TABLE)
        if part != 1:
            weight = lookup(table, scalar_ref[1])[:, :1] / 1024.0
        for n in range(width // tile):
            columns = pl.ds(n * tile, tile)

            def product(ref):
                if part == 1:
                    return jnp.dot(both(0, half), ref[0, near, columns], preferred_element_type=F32)
                if part == 2:
                    return jnp.dot(both(0, half), ref[0, far, columns], preferred_element_type=F32)
                value = jnp.dot(both(0, half), ref[0, near, columns], preferred_element_type=F32)
                return value + jnp.dot(
                    both(half + TABLE, half), ref[0, far, columns], preferred_element_type=F32
                )

            g, u = product(gate_ref), product(up_ref)
            if part == 1:
                refs[-2][:, columns] = g
                refs[-1][:, columns] = u
                continue
            if part == 2:
                g += refs[0][:, columns]
                u += refs[1][:, columns]
            refs[-1][:, columns] = (g / (1.0 + jnp.exp(-g)) * u * weight).astype(BF)

    shape = lambda kind: jax.ShapeDtypeStruct((2 * rows, width), kind)
    out = (shape(F32), shape(F32)) if part == 1 else shape(BF)
    return call(kernel, out, [scalars, keep, got, gate, up, *first, *tokens])


def down(scalars, hidden, weights, part, parts, *tokens):
    rows, depth = hidden.shape
    size = rows // 2 // parts
    tile = weights.shape[2] // 2

    def kernel(scalar_ref, hidden_ref, down_ref, *refs):
        near, away = refs[-2:]
        x = scalar_ref[0]
        value = jnp.concatenate(
            [hidden_ref[start : start + size] for start in (part * size, rows // 2 + part * size)], axis=0
        )
        for n in range(2):
            side = x if n else 1 - x
            weight = down_ref[0, :, pl.ds(pl.multiple_of(side * tile, 128), tile)]
            got = jnp.dot(value, weight, preferred_element_type=F32).astype(BF)
            near[n] = got[:size]
            away[n] = got[size:]

    out = jax.ShapeDtypeStruct((2, size, tile), BF)
    return call(kernel, (out, out), [scalars, hidden, weights, *tokens])


def spread(me, put, near, back, first, apart):
    rows, room = put.shape[1], put.shape[2] // 2
    width = near.shape[2]
    shape = lambda count: jax.ShapeDtypeStruct((count, rows, width), BF)

    def kernel(me_ref, put_ref, near_ref, back_ref, *outs):
        give, keep = (outs[0], outs[1]) if apart else (outs[0].at[0:2], outs[0].at[2:4])
        core = me_ref[0] % NC
        got = {}
        for h in range(2):
            for j in range(NY):
                part = pl.ds(j * room, room)
                value = jnp.concatenate([near_ref[h, part], back_ref[h, part]], axis=0)
                got[h, j] = jnp.dot(put_ref[first + j], value, preferred_element_type=F32).astype(BF)
        give[0] = jnp.where(core == 0, got[0, 0], got[1, 1])
        give[1] = got[0, 1]
        keep[0] = got[1, 0]
        keep[1] = jnp.where(core == 0, got[1, 1], got[0, 0])

    return call(kernel, (shape(2), shape(2)) if apart else shape(4), [me.reshape(1), put, near, back])


def in_order(values, earlier):
    return lax.optimization_barrier((*values, *earlier))[: len(values)]


def after(value, *earlier):
    return in_order((value,), earlier)[0]


def add(*values):
    total = values[0].astype(F32)
    for value in values[1:]:
        total = total + value.astype(F32)
    return total.astype(BF)


def block_mesh(tokens, expert_ids, weight_num, gate_proj, up_proj, down_proj):
    x = lax.axis_index("dp")
    me = lax.axis_index("expert")
    rows, width = tokens.shape
    half = width // 2
    room = rows * expert_ids.shape[1] // (NZ * NY * NC)

    scalars = jnp.stack([x, me])

    mine, far = prepare(x, tokens, expert_ids, weight_num)
    f1 = swap_z(far, 1, "f1")
    f0y = swap_y(far, "f0y")
    m1 = swap_z(mine, 1, "m1")
    m0y = swap_y(mine, "m0y")
    m2 = swap_z(mine, 2, "m2")
    touched = touch(*in_order((gate_proj, up_proj), (mine,)))
    f0y, m0y, m2, _ = lax.optimization_barrier((f0y, m0y, m2, touched))
    r2 = swap_xy(m2, False, "r2")
    q2 = swap_xy(m2, True, "q2")
    m3 = swap_z(m2, 1, "m3")
    keep_0, give, put_0, w0y = select(after(me, m2), room, half, [(mine, far), (m0y, f0y)], True, MUCH)
    got_0 = swap_core(after(give, q2, f1, m1), "rows_0")
    w1y = swap_z(w0y, 1, "w1y")
    q2, r2, m3 = lax.optimization_barrier((q2, r2, m3))
    t2 = swap_xy(q2, False, "t2")
    r3 = swap_xy(m3, False, "r3")
    q3 = swap_xy(m3, True, "q3")
    t3 = swap_xy(q3, False, "t3")
    hidden_0 = gate_up(after(scalars, m3), keep_0, got_0, gate_proj, up_proj, 0)
    near_0, away = down(scalars, hidden_0, down_proj, 0, 1)
    back_0 = swap_core(away, "back_0")

    blocks = [(m2,), ((r2, q2),), (m3,), ((r3, q3),)]
    keep, give, put = select(after(me, near_0, w1y, t2, r3, q3), room, half, blocks, False, MUCH)
    got = swap_core(give, "rows_m")
    keep_1, give, put_1 = select(after(me, keep), room, half, [(m1, f1), (w1y,)])
    got_1 = swap_core(give, "rows_1")
    first = gate_up(after(scalars, keep_1), keep, got, gate_proj, up_proj, 1)
    keep_f, give_f = select_far(me, after(put, first[0]), half, [(q2, r2), t2, (q3, r3), t3])
    got_f = swap_core(give_f, "rows_f")
    hidden_1 = gate_up(after(scalars, keep_f), keep_1, got_1, gate_proj, up_proj, 0)
    near_1, away = down(scalars, hidden_1, down_proj, 0, 1)
    back_1 = swap_core(away, "back_1")
    hidden = gate_up(after(scalars, near_1), keep_f, got_f, gate_proj, up_proj, 2, [*first, keep, got])
    near_3, away = down(scalars, hidden, down_proj, 1, 2, touched)
    back_3 = swap_core(away, "back_3")
    k1 = spread(me, after(put_1, near_3), near_1, back_1, 0, False)
    near_2, away = down(after(scalars, k1), hidden, down_proj, 0, 2)
    back_2 = swap_core(away, "back_2")
    give_3, keep_3 = spread(me, after(put, near_2), near_3, back_3, 2, True)
    give_2, keep_2 = spread(me, after(put, keep_3), near_2, back_2, 0, True)
    own = spread(me, after(put_0, keep_2), near_0, back_0, 0, False)

    n = swap_z(k1, 1, "n")
    u3 = swap_xy(give_3, True, "u3")
    u3 = add(keep_3, after(u3, keep_2))
    v3 = swap_xy(u3[1], False, "v3")
    u2 = swap_xy(give_2, True, "u2")
    u2 = add(keep_2, after(u2, u3))
    v2 = swap_xy(u2[1], False, "v2")
    s3 = add(u3[0], after(v3, u2))
    n = add(own, after(n, s3))
    s3 = swap_z(s3, 1, "s3")
    s2 = add(u2[0], v2, s3)
    u0 = swap_xy(n[:2], True, "u0")
    s2 = swap_z(s2, 2, "s2")
    u0 = add(n[2:], u0)
    v0 = swap_xy(u0[1], False, "v0")
    return add(u0[0], v0, s2)


def solution(mesh):
    placed = (
        P("expert", None),
        P("expert", None),
        P("expert", None),
        P("expert", None, "dp"),
        P("expert", None, "dp"),
        P("expert", "dp", None),
    )
    blocked = mesh.shape["dp"] == 2 and mesh.shape["expert"] == NZ * NY * NC
    return jax.shard_map(
        block_mesh if blocked else any_mesh,
        mesh=mesh,
        in_specs=placed,
        out_specs=P("expert", "dp"),
        check_vma=False,
    )
```

```python
import jax
import jax.numpy as jnp
from jax import lax
from jax.experimental import pallas as pl
from jax.experimental.pallas import tpu as pltpu
from jax.sharding import PartitionSpec as P

ROOM = 8
BF = jnp.bfloat16
F32 = jnp.float32


def routing_table(block_ids, expert_total, capacity):
    row_count = block_ids.shape[0]
    top_count = block_ids.shape[1]
    flat_ids = block_ids.reshape(-1)
    onehot = (flat_ids[:, None] == jnp.arange(expert_total, dtype=jnp.int32)[None, :]).astype(
        jnp.int32
    )
    before = jnp.cumsum(onehot, axis=0) - onehot
    position = jnp.sum(before * onehot, axis=1)
    target = flat_ids * capacity + position
    owners = jnp.full((expert_total * capacity,), row_count * top_count, jnp.int32)
    owners = owners.at[target].set(jnp.arange(row_count * top_count, dtype=jnp.int32))
    return (target, owners)


def any_mesh(tokens, expert_ids, weight_num, gate_proj, up_proj, down_proj):
    experts = lax.axis_size("expert")
    row_count, top_count = expert_ids.shape
    feature_width = tokens.shape[1]
    capacity = max(ROOM, (row_count * top_count + experts - 1) // experts)
    target, owners = routing_table(expert_ids, experts, capacity)
    usable = owners < row_count * top_count
    source_row = jnp.where(usable, owners // top_count, 0)
    outgoing = jnp.where(usable[:, None], tokens[source_row], jnp.zeros((), tokens.dtype))
    outgoing = outgoing.reshape(experts, capacity, feature_width)
    block_rows = lax.all_to_all(outgoing, "expert", split_axis=0, concat_axis=0, tiled=True)
    flat_rows = block_rows.reshape(-1, feature_width)
    gate_out = jnp.dot(flat_rows, gate_proj[0], preferred_element_type=F32)
    up_out = jnp.dot(flat_rows, up_proj[0], preferred_element_type=F32)
    hidden = (jax.nn.silu(gate_out) * up_out).astype(BF)
    share_out = jnp.dot(hidden, down_proj[0], preferred_element_type=F32).astype(BF)
    partial_value = share_out.reshape(block_rows.shape[0], block_rows.shape[1], feature_width)
    weights = weight_num.astype(F32) / 1024.0
    summed = lax.psum_scatter(partial_value, "dp", scatter_dimension=2, tiled=True)
    returned = lax.all_to_all(summed, "expert", split_axis=0, concat_axis=0, tiled=True)
    part_width = returned.shape[2]
    picked = returned.astype(F32).reshape(experts * capacity, part_width)[target].reshape(
        row_count, top_count, part_width
    )
    return jnp.sum(picked * weights[:, :, None], axis=1).astype(BF)


NZ, NY, NC = 4, 2, 2
TABLE = 128
SMALL = 16
KJ = [(k, j) for k in range(NZ) for j in range(NY)]


def swap_expert(value, flip, name):
    pairs = [(i, i ^ flip) for i in range(NZ * NY * NC)]
    with jax.named_scope(name):
        return lax.ppermute(value, "expert", pairs)


def swap_z(value, k, name):
    return swap_expert(value, k * NY * NC, name)


def swap_y(value, name):
    return swap_expert(value, NC, name)


def swap_core(value, name):
    return swap_expert(value, 1, name)


def swap_x(value, name):
    with jax.named_scope(name):
        return lax.ppermute(value, "dp", [(0, 1), (1, 0)])


def swap_xy(value, first, name):
    pairs = []
    experts = NZ * NY * NC
    for x in range(2):
        for e in range(experts):
            along_x = (e % NC == 0) == first
            pairs.append((x * experts + e, (1 - x) * experts + e if along_x else x * experts + (e ^ NC)))
    with jax.named_scope(name):
        return lax.ppermute(value, ("dp", "expert"), pairs)


COST = pl.CostEstimate(flops=1, bytes_accessed=1, transcendentals=0)
MUCH = pl.CostEstimate(flops=1 << 35, bytes_accessed=1, transcendentals=0)


def call(kernel, out, ins, cost=COST):
    spec = [
        pl.BlockSpec(memory_space=pltpu.SMEM if v.dtype == jnp.int32 else pltpu.VMEM) for v in ins
    ]
    return pl.pallas_call(
        kernel,
        out_shape=out,
        in_specs=spec,
        out_specs=jax.tree.map(lambda _: pl.BlockSpec(memory_space=pltpu.VMEM), out),
        compiler_params=pltpu.CompilerParams(vmem_limit_bytes=SMALL << 20),
        cost_estimate=cost,
    )(*ins)


def prepare(x, tokens, ids, numerators):
    rows, width = tokens.shape
    half = width // 2

    def kernel(x_ref, tokens_ref, ids_ref, numerators_ref, mine, far):
        side = x_ref[0]
        mine[:, :half] = tokens_ref[:, pl.ds(pl.multiple_of(side * half, 128), half)]
        far[...] = tokens_ref[:, pl.ds(pl.multiple_of((1 - side) * half, 128), half)]
        column = lax.broadcasted_iota(jnp.int32, (TABLE, rows), 0)
        expert = jnp.where(column < TABLE // 2, column, column - TABLE // 2)
        total = jnp.zeros((TABLE, rows), jnp.int32)
        for k in range(ids_ref.shape[0]):
            total += jnp.where(expert == ids_ref[pl.ds(k, 1)], numerators_ref[pl.ds(k, 1)], 0)
        high = lax.shift_right_logical(total, 5)
        code = jnp.where(column < TABLE // 2, high, total - high * 32)
        mine[:, half:] = code.astype(F32).T.astype(BF)

    out = (
        jax.ShapeDtypeStruct((rows, half + TABLE), BF),
        jax.ShapeDtypeStruct((rows, half), BF),
    )
    vmem = pl.BlockSpec(memory_space=pltpu.VMEM)
    return pl.pallas_call(
        kernel,
        out_shape=out,
        in_specs=[pl.BlockSpec(memory_space=pltpu.SMEM), vmem, vmem, vmem],
        out_specs=(vmem, vmem),
        cost_estimate=COST,
    )(x.reshape(1), tokens, ids.T, numerators.T)


def lookup(table, expert):
    row = lax.broadcasted_iota(jnp.int32, (TABLE, TABLE), 0)
    whose = jnp.where(lax.broadcasted_iota(jnp.int32, (TABLE, TABLE), 1) == 0, expert, expert + 1 - 2 * (expert % 2))
    code = jnp.where(row == whose, 32.0, 0.0) + jnp.where(row == whose + TABLE // 2, 1.0, 0.0)
    return jnp.dot(table, code.astype(BF), preferred_element_type=F32)


def chooser(refs, layout, core):
    def read(n, columns=slice(None)):
        piece = layout[n]
        if isinstance(piece, tuple):
            return jnp.where(core == 0, refs[piece[0]][:, columns], refs[piece[1]][:, columns])
        return refs[piece][:, columns]

    return read


def flatten(pieces):
    arrays, layout = [], []

    def number(array):
        for n, other in enumerate(arrays):
            if other is array:
                return n
        arrays.append(array)
        return len(arrays) - 1

    for piece in pieces:
        layout.append(tuple(number(p) for p in piece) if isinstance(piece, tuple) else number(piece))
    return arrays, layout


def select(me, room, half, blocks, join=False, cost=COST):
    count = len(blocks)
    rows = blocks[0][0].shape[0]
    arrays, layout = flatten([piece for block in blocks for piece in block])
    widths = [arrays[n[0] if isinstance(n, tuple) else n].shape[1] for n in layout]
    start_of = [sum(len(block) for block in blocks[:b]) for b in range(count)]
    full = sum(widths[: len(blocks[0])])

    def kernel(me_ref, *refs):
        keep, give, put_ref = refs[-4:-1] if join else refs[-3:]
        mine = me_ref[0]
        read = chooser(refs, layout, mine % NC)
        before = lax.broadcasted_iota(jnp.int32, (rows, rows), 1) < lax.broadcasted_iota(
            jnp.int32, (rows, rows), 0
        )
        before = jnp.where(before, 1.0, 0.0).astype(BF)
        slot = lax.broadcasted_iota(jnp.int32, (rows, 2 * room), 1)
        first = slot < room
        tables = [read(n, slice(half, half + TABLE)) for n in start_of]
        chosen = [jnp.where(lookup(table, mine) > 0, 1.0, 0.0) for table in tables]
        place = [jnp.dot(before, c.astype(BF), preferred_element_type=F32) for c in chosen]
        put = []
        for c, p in zip(chosen, place, strict=True):
            want = jnp.where(first, p[:, :1], p[:, 1:2] + room)
            here = jnp.where(first, c[:, :1], c[:, 1:2])
            put.append(jnp.where(want == slot.astype(F32), here, 0.0))
        pick = [p.T.astype(BF) for p in put]
        for b in range(count):
            put_ref[b] = put[b].astype(BF)
            start = 0
            for n in range(start_of[b], start_of[b] + len(blocks[b])):
                columns = slice(start, start + widths[n])
                value = read(n)
                got = jnp.dot(pick[b], value, preferred_element_type=F32).astype(BF)
                keep[pl.ds(b * room, room), columns] = got[:room]
                give[pl.ds(b * room, room), columns] = got[room:]
                if join and b == count - 1:
                    refs[-1][:, columns] = value
                start += widths[n]

    out = jax.ShapeDtypeStruct((count * room, full), BF)
    put = jax.ShapeDtypeStruct((count, rows, 2 * room), BF)
    last = (jax.ShapeDtypeStruct((rows, full), BF),) if join else ()
    return call(kernel, (out, out, put, *last), [me.reshape(1), *arrays], cost)


def select_far(me, put, half, pieces):
    rows = put.shape[1]
    room = put.shape[2] // 2
    arrays, layout = flatten(pieces)

    def kernel(me_ref, put_ref, *refs):
        keep, give = refs[-2:]
        read = chooser(refs, layout, me_ref[0] % NC)
        for b in range(len(pieces)):
            pick = put_ref[b].astype(F32).T.astype(BF)
            got = jnp.dot(pick, read(b, slice(0, half)), preferred_element_type=F32).astype(BF)
            keep[pl.ds(b * room, room)] = got[:room]
            give[pl.ds(b * room, room)] = got[room:]

    out = jax.ShapeDtypeStruct((len(pieces) * room, half), BF)
    return call(kernel, (out, out), [me.reshape(1), put, *arrays])


def touch(*weights):
    def kernel(*refs):
        total = jnp.zeros((16, 128), F32)
        for ref in refs[:-1]:
            total += ref[0, :16, :128].astype(F32)
        refs[-1][...] = total

    return call(kernel, jax.ShapeDtypeStruct((16, 128), F32), weights)


def gate_up(scalars, keep, got, gate, up, part, first=(), tokens=()):
    rows = keep.shape[0]
    depth, width = gate.shape[1:]
    half = depth // 2
    tile = 256

    def kernel(scalar_ref, keep_ref, got_ref, gate_ref, up_ref, *refs):
        x = scalar_ref[0]
        near = pl.ds(pl.multiple_of(x * half, half), half)
        far = pl.ds(pl.multiple_of((1 - x) * half, half), half)
        both = lambda start, size: jnp.concatenate(
            [ref[:, start : start + size] for ref in (keep_ref, got_ref)], axis=0
        )
        if part == 2:
            table = jnp.concatenate([refs[2][...], refs[3][...]], axis=0)[:, half:]
        elif part == 0:
            table = both(half, TABLE)
        if part != 1:
            weight = lookup(table, scalar_ref[1])[:, :1] / 1024.0
        for n in range(width // tile):
            columns = pl.ds(n * tile, tile)

            def product(ref):
                if part == 1:
                    return jnp.dot(both(0, half), ref[0, near, columns], preferred_element_type=F32)
                if part == 2:
                    return jnp.dot(both(0, half), ref[0, far, columns], preferred_element_type=F32)
                value = jnp.dot(both(0, half), ref[0, near, columns], preferred_element_type=F32)
                return value + jnp.dot(
                    both(half + TABLE, half), ref[0, far, columns], preferred_element_type=F32
                )

            g, u = product(gate_ref), product(up_ref)
            if part == 1:
                refs[-2][:, columns] = g
                refs[-1][:, columns] = u
                continue
            if part == 2:
                g += refs[0][:, columns]
                u += refs[1][:, columns]
            refs[-1][:, columns] = (g / (1.0 + jnp.exp(-g)) * u * weight).astype(BF)

    shape = lambda kind: jax.ShapeDtypeStruct((2 * rows, width), kind)
    out = (shape(F32), shape(F32)) if part == 1 else shape(BF)
    return call(kernel, out, [scalars, keep, got, gate, up, *first, *tokens])


def down(scalars, hidden, weights, part, parts, *tokens):
    rows, depth = hidden.shape
    size = rows // 2 // parts
    tile = weights.shape[2] // 2

    def kernel(scalar_ref, hidden_ref, down_ref, *refs):
        near, away = refs[-2:]
        x = scalar_ref[0]
        value = jnp.concatenate(
            [hidden_ref[start : start + size] for start in (part * size, rows // 2 + part * size)], axis=0
        )
        for n in range(2):
            side = x if n else 1 - x
            weight = down_ref[0, :, pl.ds(pl.multiple_of(side * tile, 128), tile)]
            got = jnp.dot(value, weight, preferred_element_type=F32).astype(BF)
            near[n] = got[:size]
            away[n] = got[size:]

    out = jax.ShapeDtypeStruct((2, size, tile), BF)
    return call(kernel, (out, out), [scalars, hidden, weights, *tokens])


def spread(me, put, near, back, first, apart):
    rows, room = put.shape[1], put.shape[2] // 2
    width = near.shape[2]
    shape = lambda count: jax.ShapeDtypeStruct((count, rows, width), BF)

    def kernel(me_ref, put_ref, near_ref, back_ref, *outs):
        give, keep = (outs[0], outs[1]) if apart else (outs[0].at[0:2], outs[0].at[2:4])
        core = me_ref[0] % NC
        got = {}
        for h in range(2):
            for j in range(NY):
                part = pl.ds(j * room, room)
                value = jnp.concatenate([near_ref[h, part], back_ref[h, part]], axis=0)
                got[h, j] = jnp.dot(put_ref[first + j], value, preferred_element_type=F32).astype(BF)
        give[0] = jnp.where(core == 0, got[0, 0], got[1, 1])
        give[1] = got[0, 1]
        keep[0] = got[1, 0]
        keep[1] = jnp.where(core == 0, got[1, 1], got[0, 0])

    return call(kernel, (shape(2), shape(2)) if apart else shape(4), [me.reshape(1), put, near, back])


def in_order(values, earlier):
    return lax.optimization_barrier((*values, *earlier))[: len(values)]


def after(value, *earlier):
    return in_order((value,), earlier)[0]


def add(*values):
    total = values[0].astype(F32)
    for value in values[1:]:
        total = total + value.astype(F32)
    return total.astype(BF)


def block_mesh(tokens, expert_ids, weight_num, gate_proj, up_proj, down_proj):
    x = lax.axis_index("dp")
    me = lax.axis_index("expert")
    rows, width = tokens.shape
    half = width // 2
    room = rows * expert_ids.shape[1] // (NZ * NY * NC)

    scalars = jnp.stack([x, me])

    mine, far = prepare(x, tokens, expert_ids, weight_num)
    f1 = swap_z(far, 1, "f1")
    f0y = swap_y(far, "f0y")
    m1 = swap_z(mine, 1, "m1")
    m0y = swap_y(mine, "m0y")
    m2 = swap_z(mine, 2, "m2")
    touched = touch(*in_order((gate_proj, up_proj), (mine,)))
    f0y, m0y, m2, _ = lax.optimization_barrier((f0y, m0y, m2, touched))
    r2 = swap_xy(m2, False, "r2")
    q2 = swap_xy(m2, True, "q2")
    m3 = swap_z(m2, 1, "m3")
    keep_0, give, put_0, w0y = select(after(me, m2), room, half, [(mine, far), (m0y, f0y)], True, MUCH)
    got_0 = swap_core(after(give, q2, f1, m1), "rows_0")
    w1y = swap_z(w0y, 1, "w1y")
    q2, r2, m3 = lax.optimization_barrier((q2, r2, m3))
    t2 = swap_xy(q2, False, "t2")
    r3 = swap_xy(m3, False, "r3")
    q3 = swap_xy(m3, True, "q3")
    t3 = swap_xy(q3, False, "t3")
    hidden_0 = gate_up(after(scalars, m3), keep_0, got_0, gate_proj, up_proj, 0)
    near_0, away = down(scalars, hidden_0, down_proj, 0, 1)
    back_0 = swap_core(away, "back_0")

    blocks = [(m2,), ((r2, q2),), (m3,), ((r3, q3),)]
    keep, give, put = select(after(me, near_0, w1y, t2, r3, q3), room, half, blocks, False, MUCH)
    got = swap_core(give, "rows_m")
    keep_1, give, put_1 = select(after(me, keep), room, half, [(m1, f1), (w1y,)])
    got_1 = swap_core(give, "rows_1")
    first = gate_up(after(scalars, keep_1), keep, got, gate_proj, up_proj, 1)
    keep_f, give_f = select_far(me, after(put, first[0]), half, [(q2, r2), t2, (q3, r3), t3])
    got_f = swap_core(give_f, "rows_f")
    hidden_1 = gate_up(after(scalars, keep_f), keep_1, got_1, gate_proj, up_proj, 0)
    near_1, away = down(scalars, hidden_1, down_proj, 0, 1)
    back_1 = swap_core(away, "back_1")
    hidden = gate_up(after(scalars, near_1), keep_f, got_f, gate_proj, up_proj, 2, [*first, keep, got])
    near_3, away = down(scalars, hidden, down_proj, 1, 2, touched)
    back_3 = swap_core(away, "back_3")
    give_1, keep_1 = spread(me, after(put_1, near_3), near_1, back_1, 0, True)
    near_2, away = down(after(scalars, keep_1), hidden, down_proj, 0, 2)
    back_2 = swap_core(away, "back_2")
    give_3, keep_3 = spread(me, after(put, near_2), near_3, back_3, 2, True)
    give_2, keep_2 = spread(me, after(put, keep_3), near_2, back_2, 0, True)
    give_0, keep_0 = spread(me, after(put_0, keep_2), near_0, back_0, 0, True)

    nk = swap_z(keep_1, 1, "nk")
    u3 = swap_xy(give_3, True, "u3")
    ng = swap_z(give_1, 1, "ng")
    u3 = add(keep_3, after(u3, keep_2, ng))
    v3 = swap_xy(u3[1], False, "v3")
    u2 = swap_xy(give_2, True, "u2")
    u2 = add(keep_2, after(u2, u3))
    v2 = swap_xy(u2[1], False, "v2")
    s3 = add(u3[0], after(v3, u2))
    ng = add(give_0, after(ng, s3))
    nk = add(keep_0, after(nk, s3))
    s3 = swap_z(s3, 1, "s3")
    s2 = add(u2[0], v2, s3)
    u0 = swap_xy(ng, True, "u0")
    s2 = swap_z(s2, 2, "s2")
    u0 = add(nk, u0)
    v0 = swap_xy(u0[1], False, "v0")
    return add(u0[0], v0, s2)


def solution(mesh):
    placed = (
        P("expert", None),
        P("expert", None),
        P("expert", None),
        P("expert", None, "dp"),
        P("expert", None, "dp"),
        P("expert", "dp", None),
    )
    blocked = mesh.shape["dp"] == 2 and mesh.shape["expert"] == NZ * NY * NC
    return jax.shard_map(
        block_mesh if blocked else any_mesh,
        mesh=mesh,
        in_specs=placed,
        out_specs=P("expert", "dp"),
        check_vma=False,
    )
```

```python
import jax
import jax.numpy as jnp
from jax import lax
from jax.experimental import pallas as pl
from jax.experimental.pallas import tpu as pltpu
from jax.sharding import PartitionSpec as P

ROOM = 8
BF = jnp.bfloat16
F32 = jnp.float32


def routing_table(block_ids, expert_total, capacity):
    row_count = block_ids.shape[0]
    top_count = block_ids.shape[1]
    flat_ids = block_ids.reshape(-1)
    onehot = (flat_ids[:, None] == jnp.arange(expert_total, dtype=jnp.int32)[None, :]).astype(
        jnp.int32
    )
    before = jnp.cumsum(onehot, axis=0) - onehot
    position = jnp.sum(before * onehot, axis=1)
    target = flat_ids * capacity + position
    owners = jnp.full((expert_total * capacity,), row_count * top_count, jnp.int32)
    owners = owners.at[target].set(jnp.arange(row_count * top_count, dtype=jnp.int32))
    return (target, owners)


def any_mesh(tokens, expert_ids, weight_num, gate_proj, up_proj, down_proj):
    experts = lax.axis_size("expert")
    row_count, top_count = expert_ids.shape
    feature_width = tokens.shape[1]
    capacity = max(ROOM, (row_count * top_count + experts - 1) // experts)
    target, owners = routing_table(expert_ids, experts, capacity)
    usable = owners < row_count * top_count
    source_row = jnp.where(usable, owners // top_count, 0)
    outgoing = jnp.where(usable[:, None], tokens[source_row], jnp.zeros((), tokens.dtype))
    outgoing = outgoing.reshape(experts, capacity, feature_width)
    block_rows = lax.all_to_all(outgoing, "expert", split_axis=0, concat_axis=0, tiled=True)
    flat_rows = block_rows.reshape(-1, feature_width)
    gate_out = jnp.dot(flat_rows, gate_proj[0], preferred_element_type=F32)
    up_out = jnp.dot(flat_rows, up_proj[0], preferred_element_type=F32)
    hidden = (jax.nn.silu(gate_out) * up_out).astype(BF)
    share_out = jnp.dot(hidden, down_proj[0], preferred_element_type=F32).astype(BF)
    partial_value = share_out.reshape(block_rows.shape[0], block_rows.shape[1], feature_width)
    weights = weight_num.astype(F32) / 1024.0
    summed = lax.psum_scatter(partial_value, "dp", scatter_dimension=2, tiled=True)
    returned = lax.all_to_all(summed, "expert", split_axis=0, concat_axis=0, tiled=True)
    part_width = returned.shape[2]
    picked = returned.astype(F32).reshape(experts * capacity, part_width)[target].reshape(
        row_count, top_count, part_width
    )
    return jnp.sum(picked * weights[:, :, None], axis=1).astype(BF)


NZ, NY, NC = 4, 2, 2
TABLE = 128
SMALL = 16
KJ = [(k, j) for k in range(NZ) for j in range(NY)]


def swap_expert(value, flip, name):
    pairs = [(i, i ^ flip) for i in range(NZ * NY * NC)]
    with jax.named_scope(name):
        return lax.ppermute(value, "expert", pairs)


def swap_z(value, k, name):
    return swap_expert(value, k * NY * NC, name)


def swap_y(value, name):
    return swap_expert(value, NC, name)


def swap_core(value, name):
    return swap_expert(value, 1, name)


def swap_x(value, name):
    with jax.named_scope(name):
        return lax.ppermute(value, "dp", [(0, 1), (1, 0)])


def swap_xy(value, first, name):
    pairs = []
    experts = NZ * NY * NC
    for x in range(2):
        for e in range(experts):
            along_x = (e % NC == 0) == first
            pairs.append((x * experts + e, (1 - x) * experts + e if along_x else x * experts + (e ^ NC)))
    with jax.named_scope(name):
        return lax.ppermute(value, ("dp", "expert"), pairs)


COST = pl.CostEstimate(flops=1, bytes_accessed=1, transcendentals=0)
MUCH = pl.CostEstimate(flops=1 << 35, bytes_accessed=1, transcendentals=0)


def call(kernel, out, ins, cost=COST):
    spec = [
        pl.BlockSpec(memory_space=pltpu.SMEM if v.dtype == jnp.int32 else pltpu.VMEM) for v in ins
    ]
    return pl.pallas_call(
        kernel,
        out_shape=out,
        in_specs=spec,
        out_specs=jax.tree.map(lambda _: pl.BlockSpec(memory_space=pltpu.VMEM), out),
        compiler_params=pltpu.CompilerParams(vmem_limit_bytes=SMALL << 20),
        cost_estimate=cost,
    )(*ins)


def prepare(x, tokens, ids, numerators):
    rows, width = tokens.shape
    half = width // 2

    def kernel(x_ref, tokens_ref, ids_ref, numerators_ref, mine, far):
        side = x_ref[0]
        mine[:, :half] = tokens_ref[:, pl.ds(pl.multiple_of(side * half, 128), half)]
        far[...] = tokens_ref[:, pl.ds(pl.multiple_of((1 - side) * half, 128), half)]
        column = lax.broadcasted_iota(jnp.int32, (TABLE, rows), 0)
        expert = jnp.where(column < TABLE // 2, column, column - TABLE // 2)
        total = jnp.zeros((TABLE, rows), jnp.int32)
        for k in range(ids_ref.shape[0]):
            total += jnp.where(expert == ids_ref[pl.ds(k, 1)], numerators_ref[pl.ds(k, 1)], 0)
        high = lax.shift_right_logical(total, 5)
        code = jnp.where(column < TABLE // 2, high, total - high * 32)
        mine[:, half:] = code.astype(F32).T.astype(BF)

    out = (
        jax.ShapeDtypeStruct((rows, half + TABLE), BF),
        jax.ShapeDtypeStruct((rows, half), BF),
    )
    vmem = pl.BlockSpec(memory_space=pltpu.VMEM)
    return pl.pallas_call(
        kernel,
        out_shape=out,
        in_specs=[pl.BlockSpec(memory_space=pltpu.SMEM), vmem, vmem, vmem],
        out_specs=(vmem, vmem),
        cost_estimate=COST,
    )(x.reshape(1), tokens, ids.T, numerators.T)


def lookup(table, expert):
    row = lax.broadcasted_iota(jnp.int32, (TABLE, TABLE), 0)
    whose = jnp.where(lax.broadcasted_iota(jnp.int32, (TABLE, TABLE), 1) == 0, expert, expert + 1 - 2 * (expert % 2))
    code = jnp.where(row == whose, 32.0, 0.0) + jnp.where(row == whose + TABLE // 2, 1.0, 0.0)
    return jnp.dot(table, code.astype(BF), preferred_element_type=F32)


def chooser(refs, layout, core):
    def read(n, columns=slice(None)):
        piece = layout[n]
        if isinstance(piece, tuple):
            return jnp.where(core == 0, refs[piece[0]][:, columns], refs[piece[1]][:, columns])
        return refs[piece][:, columns]

    return read


def flatten(pieces):
    arrays, layout = [], []

    def number(array):
        for n, other in enumerate(arrays):
            if other is array:
                return n
        arrays.append(array)
        return len(arrays) - 1

    for piece in pieces:
        layout.append(tuple(number(p) for p in piece) if isinstance(piece, tuple) else number(piece))
    return arrays, layout


def select(me, room, half, blocks, join=False, cost=COST):
    count = len(blocks)
    rows = blocks[0][0].shape[0]
    arrays, layout = flatten([piece for block in blocks for piece in block])
    widths = [arrays[n[0] if isinstance(n, tuple) else n].shape[1] for n in layout]
    start_of = [sum(len(block) for block in blocks[:b]) for b in range(count)]
    full = sum(widths[: len(blocks[0])])

    def kernel(me_ref, *refs):
        keep, give, put_ref = refs[-4:-1] if join else refs[-3:]
        mine = me_ref[0]
        read = chooser(refs, layout, mine % NC)
        before = lax.broadcasted_iota(jnp.int32, (rows, rows), 1) < lax.broadcasted_iota(
            jnp.int32, (rows, rows), 0
        )
        before = jnp.where(before, 1.0, 0.0).astype(BF)
        slot = lax.broadcasted_iota(jnp.int32, (rows, 2 * room), 1)
        first = slot < room
        tables = [read(n, slice(half, half + TABLE)) for n in start_of]
        chosen = [jnp.where(lookup(table, mine) > 0, 1.0, 0.0) for table in tables]
        place = [jnp.dot(before, c.astype(BF), preferred_element_type=F32) for c in chosen]
        put = []
        for c, p in zip(chosen, place, strict=True):
            want = jnp.where(first, p[:, :1], p[:, 1:2] + room)
            here = jnp.where(first, c[:, :1], c[:, 1:2])
            put.append(jnp.where(want == slot.astype(F32), here, 0.0))
        pick = [p.T.astype(BF) for p in put]
        for b in range(count):
            put_ref[b] = put[b].astype(BF)
            start = 0
            for n in range(start_of[b], start_of[b] + len(blocks[b])):
                columns = slice(start, start + widths[n])
                value = read(n)
                got = jnp.dot(pick[b], value, preferred_element_type=F32).astype(BF)
                keep[pl.ds(b * room, room), columns] = got[:room]
                give[pl.ds(b * room, room), columns] = got[room:]
                if join and b == count - 1:
                    refs[-1][:, columns] = value
                start += widths[n]

    out = jax.ShapeDtypeStruct((count * room, full), BF)
    put = jax.ShapeDtypeStruct((count, rows, 2 * room), BF)
    last = (jax.ShapeDtypeStruct((rows, full), BF),) if join else ()
    return call(kernel, (out, out, put, *last), [me.reshape(1), *arrays], cost)


def select_far(me, put, half, pieces):
    rows = put.shape[1]
    room = put.shape[2] // 2
    arrays, layout = flatten(pieces)

    def kernel(me_ref, put_ref, *refs):
        keep, give = refs[-2:]
        read = chooser(refs, layout, me_ref[0] % NC)
        for b in range(len(pieces)):
            pick = put_ref[b].astype(F32).T.astype(BF)
            got = jnp.dot(pick, read(b, slice(0, half)), preferred_element_type=F32).astype(BF)
            keep[pl.ds(b * room, room)] = got[:room]
            give[pl.ds(b * room, room)] = got[room:]

    out = jax.ShapeDtypeStruct((len(pieces) * room, half), BF)
    return call(kernel, (out, out), [me.reshape(1), put, *arrays])


def touch(*weights):
    def kernel(*refs):
        total = jnp.zeros((16, 128), F32)
        for ref in refs[:-1]:
            total += ref[0, :16, :128].astype(F32)
        refs[-1][...] = total

    return call(kernel, jax.ShapeDtypeStruct((16, 128), F32), weights)


def gate_up(scalars, keep, got, gate, up, part, first=(), tokens=()):
    rows = keep.shape[0]
    depth, width = gate.shape[1:]
    half = depth // 2
    tile = 256

    def kernel(scalar_ref, keep_ref, got_ref, gate_ref, up_ref, *refs):
        x = scalar_ref[0]
        near = pl.ds(pl.multiple_of(x * half, half), half)
        far = pl.ds(pl.multiple_of((1 - x) * half, half), half)
        both = lambda start, size: jnp.concatenate(
            [ref[:, start : start + size] for ref in (keep_ref, got_ref)], axis=0
        )
        if part == 2:
            table = jnp.concatenate([refs[2][...], refs[3][...]], axis=0)[:, half:]
        elif part == 0:
            table = both(half, TABLE)
        if part != 1:
            weight = lookup(table, scalar_ref[1])[:, :1] / 1024.0
        for n in range(width // tile):
            columns = pl.ds(n * tile, tile)

            def product(ref):
                if part == 1:
                    return jnp.dot(both(0, half), ref[0, near, columns], preferred_element_type=F32)
                if part == 2:
                    return jnp.dot(both(0, half), ref[0, far, columns], preferred_element_type=F32)
                value = jnp.dot(both(0, half), ref[0, near, columns], preferred_element_type=F32)
                return value + jnp.dot(
                    both(half + TABLE, half), ref[0, far, columns], preferred_element_type=F32
                )

            g, u = product(gate_ref), product(up_ref)
            if part == 1:
                refs[-2][:, columns] = g
                refs[-1][:, columns] = u
                continue
            if part == 2:
                g += refs[0][:, columns]
                u += refs[1][:, columns]
            refs[-1][:, columns] = (g / (1.0 + jnp.exp(-g)) * u * weight).astype(BF)

    shape = lambda kind: jax.ShapeDtypeStruct((2 * rows, width), kind)
    out = (shape(F32), shape(F32)) if part == 1 else shape(BF)
    return call(kernel, out, [scalars, keep, got, gate, up, *first, *tokens])


def down(scalars, hidden, weights, part, parts, *tokens):
    rows, depth = hidden.shape
    size = rows // 2 // parts
    tile = weights.shape[2] // 2

    def kernel(scalar_ref, hidden_ref, down_ref, *refs):
        near, away = refs[-2:]
        x = scalar_ref[0]
        value = jnp.concatenate(
            [hidden_ref[start : start + size] for start in (part * size, rows // 2 + part * size)], axis=0
        )
        for n in range(2):
            side = x if n else 1 - x
            weight = down_ref[0, :, pl.ds(pl.multiple_of(side * tile, 128), tile)]
            got = jnp.dot(value, weight, preferred_element_type=F32).astype(BF)
            near[n] = got[:size]
            away[n] = got[size:]

    out = jax.ShapeDtypeStruct((2, size, tile), BF)
    return call(kernel, (out, out), [scalars, hidden, weights, *tokens])


def spread(me, put, near, back, first, apart):
    rows, room = put.shape[1], put.shape[2] // 2
    width = near.shape[2]
    shape = lambda count: jax.ShapeDtypeStruct((count, rows, width), BF)

    def kernel(me_ref, put_ref, near_ref, back_ref, *outs):
        give, keep = (outs[0], outs[1]) if apart else (outs[0].at[0:2], outs[0].at[2:4])
        core = me_ref[0] % NC
        got = {}
        for h in range(2):
            for j in range(NY):
                part = pl.ds(j * room, room)
                value = jnp.concatenate([near_ref[h, part], back_ref[h, part]], axis=0)
                got[h, j] = jnp.dot(put_ref[first + j], value, preferred_element_type=F32).astype(BF)
        give[0] = jnp.where(core == 0, got[0, 0], got[1, 1])
        give[1] = got[0, 1]
        keep[0] = got[1, 0]
        keep[1] = jnp.where(core == 0, got[1, 1], got[0, 0])

    return call(kernel, (shape(2), shape(2)) if apart else shape(4), [me.reshape(1), put, near, back])


def in_order(values, earlier):
    return lax.optimization_barrier((*values, *earlier))[: len(values)]


def after(value, *earlier):
    return in_order((value,), earlier)[0]


def add(*values):
    total = values[0].astype(F32)
    for value in values[1:]:
        total = total + value.astype(F32)
    return total.astype(BF)


def block_mesh(tokens, expert_ids, weight_num, gate_proj, up_proj, down_proj):
    x = lax.axis_index("dp")
    me = lax.axis_index("expert")
    rows, width = tokens.shape
    half = width // 2
    room = rows * expert_ids.shape[1] // (NZ * NY * NC)

    scalars = jnp.stack([x, me])

    mine, far = prepare(x, tokens, expert_ids, weight_num)
    f1 = swap_z(far, 1, "f1")
    f0y = swap_y(far, "f0y")
    m1 = swap_z(mine, 1, "m1")
    m0y = swap_y(mine, "m0y")
    m2 = swap_z(mine, 2, "m2")
    touched = touch(*in_order((gate_proj, up_proj), (mine,)))
    f0y, m0y, m2, _ = lax.optimization_barrier((f0y, m0y, m2, touched))
    r2 = swap_xy(m2, False, "r2")
    q2 = swap_xy(m2, True, "q2")
    m3 = swap_z(m2, 1, "m3")
    keep_0, give, put_0, w0y = select(after(me, m2), room, half, [(mine, far), (m0y, f0y)], True, MUCH)
    got_0 = swap_core(after(give, q2, f1, m1), "rows_0")
    w1y = swap_z(w0y, 1, "w1y")
    q2, r2, m3 = lax.optimization_barrier((q2, r2, m3))
    t2 = swap_xy(q2, False, "t2")
    r3 = swap_xy(m3, False, "r3")
    q3 = swap_xy(m3, True, "q3")
    t3 = swap_xy(q3, False, "t3")
    hidden_0 = gate_up(after(scalars, m3), keep_0, got_0, gate_proj, up_proj, 0)
    near_0, away = down(scalars, hidden_0, down_proj, 0, 1)
    back_0 = swap_core(away, "back_0")

    blocks = [(m2,), ((r2, q2),), (m3,), ((r3, q3),)]
    keep, give, put = select(after(me, near_0, w1y, t2, r3, q3), room, half, blocks, False, MUCH)
    got = swap_core(give, "rows_m")
    keep_1, give, put_1 = select(after(me, keep), room, half, [(m1, f1), (w1y,)])
    got_1 = swap_core(give, "rows_1")
    first = gate_up(after(scalars, keep_1), keep, got, gate_proj, up_proj, 1)
    keep_f, give_f = select_far(me, after(put, first[0]), half, [(q2, r2), t2, (q3, r3), t3])
    got_f = swap_core(give_f, "rows_f")
    hidden_1 = gate_up(after(scalars, keep_f), keep_1, got_1, gate_proj, up_proj, 0)
    near_1, away = down(scalars, hidden_1, down_proj, 0, 1)
    back_1 = swap_core(away, "back_1")
    hidden = gate_up(after(scalars, near_1), keep_f, got_f, gate_proj, up_proj, 2, [*first, keep, got])
    near_3, away = down(scalars, hidden, down_proj, 1, 2, touched)
    back_3 = swap_core(away, "back_3")
    give_1, keep_1 = spread(me, after(put_1, near_3), near_1, back_1, 0, True)
    near_2, away = down(after(scalars, keep_1), hidden, down_proj, 0, 2)
    back_2 = swap_core(away, "back_2")
    give_3, keep_3 = spread(me, after(put, near_2), near_3, back_3, 2, True)
    give_2, keep_2 = spread(me, after(put, keep_3), near_2, back_2, 0, True)
    give_0, keep_0 = spread(me, after(put_0, keep_2), near_0, back_0, 0, True)

    nk = swap_z(keep_1, 1, "nk")
    u3 = swap_xy(give_3, True, "u3")
    ng = swap_z(give_1, 1, "ng")
    u3 = add(keep_3, after(u3, ng))
    v3 = swap_xy(u3[1], False, "v3")
    u2 = swap_xy(give_2, True, "u2")
    u2 = add(keep_2, after(u2, u3))
    v2 = swap_xy(u2[1], False, "v2")
    s3 = add(u3[0], after(v3, u2))
    ng = add(give_0, after(ng, s3))
    nk = add(keep_0, after(nk, s3))
    s3 = swap_z(s3, 1, "s3")
    s2 = add(u2[0], v2, s3)
    u0 = swap_xy(ng, True, "u0")
    s2 = swap_z(s2, 2, "s2")
    u0 = add(nk, u0)
    v0 = swap_xy(u0[1], False, "v0")
    return add(u0[0], v0, s2)


def solution(mesh):
    placed = (
        P("expert", None),
        P("expert", None),
        P("expert", None),
        P("expert", None, "dp"),
        P("expert", None, "dp"),
        P("expert", "dp", None),
    )
    blocked = mesh.shape["dp"] == 2 and mesh.shape["expert"] == NZ * NY * NC
    return jax.shard_map(
        block_mesh if blocked else any_mesh,
        mesh=mesh,
        in_specs=placed,
        out_specs=P("expert", "dp"),
        check_vma=False,
    )
```
